32 devices in a mesh: video: 2 (over y), block: 4 (over z), band: 2 (over x), chan: 2 (over core).
Axes of the slice: x: 2, y: 2, z: 4, core: 2. Of those that a mesh axis runs over, the one named last changes fastest.
Arguments:
- latents: bfloat16 [32, 2, 1664], P(('video', 'block'), 'band'), parts along dimension 0, may hold values from -60 to 60
- frame_counts: int32 [8], P('video'), parts along dimension 0, may hold values from 1 to 4, 8 in all
- w_in: bfloat16 [3, 3, 3, 16, 384], replicated, may hold values from -0.3125 to 0.3125
- gain_in: float32 [384], replicated, may hold values from 0.1 to 1.9
- shift_in: float32 [384], replicated, may hold values from -3 to 3
- w_mid: bfloat16 [3, 3, 3, 384, 384], P(None, None, None, None, 'chan'), may hold values from -0.0625 to 0.0625
- gain_out: float32 [384], P('chan'), may hold values from 0.1 to 1.9
- shift_out: float32 [384], P('chan'), may hold values from -3 to 3
Outputs:
- decoded: bfloat16 [32, 2, 104, 384], P(('video', 'block'), 'band', None, 'chan'), parts along dimension 0
The draws below stay inside these ranges and needn't reach their ends.
There are 2 independent parts, one for each index of `video`. The reference program is written for one: setup_inputs(seed, part) draws one part's arguments, and reference() takes and returns one part's arrays. A program takes and returns all parts, laid end to end along the dimension named above; an argument that names none is the same for every part. Nothing has to cross between parts.
Inputs may be any that keep to these rules, and one draw needn't show every extreme that they name: `frame_counts`: entry k is the number of consecutive latent frames that device k of the frame axis holds; the entries sum to 8.
All inputs are finite; a program needn't handle non-finite values.
Results may differ from the reference program's by a relative error of at most 0.013.
Values may be sent and summed in bfloat16 or wider, within the bound.
A program may use at most 64 MiB of HBM per device.

```python
import math
import jax
import jax.numpy as jnp
import numpy as np
from jax import lax

LAT = 16
C = 384
GROUPS = 32
COLS = 104
AVG = 2
MOST = 4
ROWS = 2
FRAMES = 8
SLOTS = 16
N_BLOCK = 4


def draw_latents(key, part):
    first_key, second_key, third_key = jax.random.split(jax.random.fold_in(key, 17), 3)
    row_place = jnp.arange(ROWS, dtype=jnp.float32)
    row_scale = jnp.exp(jax.random.uniform(second_key, (ROWS,), jnp.float32) * math.log(10.0)) / math.sqrt(10.0)
    col_scale = jnp.exp(jax.random.uniform(third_key, (COLS,), jnp.float32) * math.log(10.0)) / math.sqrt(10.0)
    base_values = jnp.clip(jax.random.normal(first_key, (SLOTS, ROWS, COLS, LAT), jnp.float32), -3.0, 3.0)
    row_scale = row_scale * jnp.sqrt(1.0 + 2.0 * row_place)
    scaled = base_values * row_scale[None, :, None, None] * col_scale[None, None, :, None]
    return scaled.reshape(SLOTS, ROWS, COLS * LAT).astype(jnp.bfloat16)


def shard_levels(own_key, dims, cuts, least, high):
    factor_of = 1.0
    for axis_at, shards_of in cuts:
        draws = jax.random.uniform(jax.random.fold_in(jax.random.fold_in(own_key, 6), axis_at), (shards_of,), jnp.float32, least / len(cuts), high / len(cuts))
        factor_of = factor_of * jnp.repeat(jnp.exp(draws), dims[axis_at] // shards_of).reshape((-1,) + (1,) * (len(dims) - 1 - axis_at))
    return factor_of


def length_profile(count, total, reach, skew):
    weights = [(1 << 20) // math.isqrt(grade ** skew) + 1 for grade in range(2, count + 1)]
    surplus, counts = total - reach - (count - 1), [1] * (count - 1)
    while surplus > 0:
        candidates = [i for i in range(count - 1) if counts[i] < reach]
        whole, left = sum([weights[i] for i in candidates]), surplus
        for i in candidates:
            extra = min(reach - counts[i], max(1, left * weights[i] // whole), surplus)
            counts[i] = counts[i] + extra
            surplus = surplus - extra
    return np.array([reach] + counts)


def ragged(key, count, total, reach, skew):
    if count == 2:
        one = jax.random.randint(key, (), max(1, total - reach), min(reach, total - 1) + 1)
        return jnp.stack([one, total - one])
    lengths = jnp.asarray(length_profile(count, total, reach, skew), jnp.int32)
    pairs = (count - 1) // 2
    donor, receiver = lengths[1:1 + 2 * pairs:2], lengths[2:2 + 2 * pairs:2]
    room = jnp.minimum(donor - 1, reach - receiver)
    moved = jax.random.randint(jax.random.fold_in(key, 1), (pairs,), 0, 1 << 20) % (room + 1)
    lengths = lengths.at[1:1 + 2 * pairs:2].set(donor - moved).at[2:2 + 2 * pairs:2].set(receiver + moved)
    return lengths[jax.random.permutation(jax.random.fold_in(key, 2), count)]


def normal_values(rng, shape, scale, limit, shards=(), kind=jnp.bfloat16):
    array = scale * jax.random.normal(rng, shape, jnp.float32)
    if shards:
        array = array * shard_levels(rng, shape, shards, -0.22, 0.18)
    return jnp.clip(array, -limit, limit).astype(kind)


def setup_inputs(seed: int = 0, part: int = 0) -> dict:
    key_list = jax.random.split(jax.random.key(seed), 9)
    part_keys = jax.random.split(jax.random.fold_in(key_list[8], part), 9)
    return {
        "latents": draw_latents(jax.random.fold_in(jax.random.fold_in(key_list[8], part), 71), part),
        "frame_counts": ragged(part_keys[1], N_BLOCK, AVG * N_BLOCK, MOST, 2).astype(jnp.int32),
        "w_in": normal_values(key_list[2], (3, 3, 3, LAT, C), (27 * LAT) ** -0.5, 0.3125),
        "gain_in": jnp.clip(1.0 + 0.18 * jax.random.normal(key_list[3], (C,), jnp.float32), 0.1, 1.9),
        "shift_in": normal_values(key_list[4], (C,), 0.5, 3.0, (), jnp.float32),
        "w_mid": normal_values(key_list[5], (3, 3, 3, C, C), (27 * C) ** -0.5, 0.0625, ((4, 2),)),
        "gain_out": jnp.clip(1.0 + 0.18 * jax.random.normal(key_list[6], (C,), jnp.float32), 0.1, 1.9),
        "shift_out": normal_values(key_list[7], (C,), 0.5, 3.0, ((0, 2),), jnp.float32),
    }


EPSILON = 1e-06

def causal_conv(inputs, kernel):
    count_in, rows_in, cols_in, width_in = inputs.shape
    out_width = kernel.shape[4]
    padded = jnp.pad(inputs, ((2, 0), (1, 1), (1, 1), (0, 0)))
    accumulate = jnp.zeros((count_in * rows_in * cols_in, out_width), jnp.float32)
    for step_t in range(3):
        for step_y in range(3):
            patches = [padded[step_t:step_t + count_in, step_y:step_y + rows_in, step_x:step_x + cols_in, :] for step_x in range(3)]
            stacked = jnp.concatenate(patches, axis=-1).reshape(-1, 3 * width_in)
            accumulate = accumulate + jnp.dot(stacked, kernel[step_t, step_y].reshape(3 * width_in, out_width), preferred_element_type=jnp.float32)
    return accumulate.reshape(count_in, rows_in, cols_in, out_width)

def group_silu(values, norm_gain, norm_shift):
    count_in = values.shape[0]
    group_width = C // GROUPS
    grouped = values.reshape(count_in, ROWS * COLS, GROUPS, group_width)
    group_total = lax.optimization_barrier(jnp.sum(grouped, axis=(1, 3)))
    squares = lax.optimization_barrier(jnp.sum(grouped * grouped, axis=(1, 3)))
    total = float(ROWS * COLS * group_width)
    group_mean = group_total / total
    variance = squares / total - group_mean * group_mean
    inverse = lax.rsqrt(variance + EPSILON)
    normed = (grouped - group_mean[:, None, :, None]) * inverse[:, None, :, None]
    normed = normed.reshape(values.shape)
    return jax.nn.silu(normed * norm_gain + norm_shift)

def reference(latents, frame_counts, w_in, gain_in, shift_in, w_mid, gain_out, shift_out):
    run_ends = jnp.cumsum(frame_counts).astype(jnp.int32)
    run_starts = (run_ends - frame_counts).astype(jnp.int32)
    frame_ids = jnp.arange(FRAMES, dtype=jnp.int32)
    owners = lax.optimization_barrier(jnp.sum((frame_ids[:, None] >= run_ends[None, :]).astype(jnp.int32), axis=1)).astype(jnp.int32)
    slot_ids = (owners * MOST + frame_ids - jnp.take(run_starts, owners)).astype(jnp.int32)
    video_frames = jnp.take(latents, slot_ids, axis=0).reshape(FRAMES, ROWS, COLS, LAT)
    first_conv = causal_conv(video_frames, w_in).astype(jnp.bfloat16)
    activated = group_silu(first_conv.astype(jnp.float32), gain_in, shift_in).astype(jnp.bfloat16)
    second_conv = causal_conv(activated, w_mid).astype(jnp.bfloat16)
    second_norm = group_silu(second_conv.astype(jnp.float32), gain_out, shift_out).astype(jnp.bfloat16)
    all_slots = jnp.arange(SLOTS, dtype=jnp.int32)
    devices_of = (all_slots // MOST).astype(jnp.int32)
    places = (all_slots % MOST).astype(jnp.int32)
    alive_mask = places < jnp.take(frame_counts, devices_of)
    sources = jnp.clip(jnp.take(run_starts, devices_of) + places, 0, FRAMES - 1).astype(jnp.int32)
    picked = jnp.take(second_norm, sources, axis=0)
    return jnp.where(alive_mask[:, None, None, None], picked, jnp.zeros_like(picked))
```

```python
import functools

import jax
import jax.numpy as jnp
from jax import lax
from jax.experimental import pallas as pl
from jax.experimental.pallas import tpu as pltpu
from jax.sharding import PartitionSpec as P

LAT = 16
C = 384
GROUPS = 32
GW = C // GROUPS
EPSILON = 1e-06
MESH = pl.DeviceIdType.MESH
F32 = jnp.float32
BF16 = jnp.bfloat16


def up(n, m):
    return (n + m - 1) // m * m


def rows_for(r, R):
    return tuple(range(max(0, r - 1), min(R - 1, r + 1) + 1))


def group_matrix(n):
    a = lax.broadcasted_iota(jnp.int32, (n, n), 0)
    b = lax.broadcasted_iota(jnp.int32, (n, n), 1)
    same = ((a * 5462) >> 16) == ((b * 5462) >> 16)
    return jnp.where(same, 1.0, 0.0).astype(BF16)


def group_sums(x, gmat):
    hi = x.astype(BF16)
    rest = x - hi.astype(F32)
    mid = rest.astype(BF16)
    lo = (rest - mid.astype(F32)).astype(BF16)
    n = x.shape[0]
    y = jnp.dot(
        jnp.concatenate([hi, mid, lo], axis=0), gmat, preferred_element_type=F32
    )
    return y[:n] + y[n : 2 * n] + y[2 * n :]


def silu(u):
    return u / (1.0 + jnp.exp(-u))


def body(
    nb, R, COLS, SL, reach,
    cnt_ref, lat_ref, win_ref, gin_ref, sin_ref, wmid_ref, gout_ref, sout_ref,
    out_ref,
    slots, xf, gf, wpad, c1s, la, lb, wv, stats,
    send_sem, recv_sem, st_send, st_recv, w_sem, win_sem,
):
    k = lax.axis_index("block")
    b = lax.axis_index("band")
    half = out_ref.shape[1]
    FL = SL + 4
    FA = SL + 2
    nin = min(3, R)
    sets = sorted(set(rows_for(r, R) for r in range(R)))

    y0 = 1 - b if R == 2 else 0
    wcopies = []
    for t in range(3):
        c = pltpu.make_async_copy(
            wmid_ref.at[t, pl.ds(y0, nin)], wv.at[t], w_sem.at[t]
        )
        wcopies.append(c)
    wincopies = []
    kpad = wpad.shape[1] // 3
    for r in range(R):
        rows = rows_for(r, R)
        first = (rows[0] - r + 1) * 3 * LAT
        size = len(rows) * 3 * LAT
        for t in range(3):
            c = pltpu.make_async_copy(
                win_ref.at[t, pl.ds(first, size)],
                wpad.at[r, pl.ds(t * kpad, size)],
                win_sem.at[r, t],
            )
            wincopies.append(c)
    barrier = pltpu.get_barrier_semaphore()
    pairs = [(d, o) for d in range(reach + 1) for o in range(R) if (d, o) != (0, 0)]
    for d, o in pairs:
        @pl.when(k >= d)
        def _():
            pl.semaphore_signal(
                barrier, inc=1,
                device_id={"block": k - d, "band": lax.rem(b + R - o, R)},
                device_id_type=MESH,
            )
    for c in wincopies:
        c.start()
    for c in wcopies:
        c.start()
    own = lat_ref[...]
    slots[0, b] = own
    for r in range(R):
        size = len(rows_for(r, R)) * 3 * LAT
        if size < kpad:
            for t in range(3):
                wpad[r, t * kpad + size : (t + 1) * kpad, :] = jnp.zeros((kpad - size, C), BF16)
    pl.semaphore_wait(barrier, jnp.minimum(reach + 1, nb - k) * R - 1)

    def copy_to(d, o):
        return pltpu.make_async_remote_copy(
            src_ref=lat_ref,
            dst_ref=slots.at[d, b],
            send_sem=send_sem.at[d, o],
            recv_sem=recv_sem.at[d, o],
            device_id={"block": k + d, "band": lax.rem(b + o, R)},
            device_id_type=MESH,
        )

    def copy_from(d, o):
        return pltpu.make_async_remote_copy(
            src_ref=lat_ref,
            dst_ref=slots.at[d, lax.rem(b + R - o, R)],
            send_sem=send_sem.at[d, o],
            recv_sem=recv_sem.at[d, o],
            device_id={"block": k, "band": lax.rem(b + o, R)},
            device_id_type=MESH,
        )

    for d, o in reversed(pairs):
        @pl.when(k + d < nb)
        def _():
            copy_to(d, o).start()

    sel = {}
    for rows in sets:
        n = len(rows)
        a = lax.broadcasted_iota(jnp.int32, (n * 3 * 128, kpad), 0)
        c = lax.broadcasted_iota(jnp.int32, (n * 3 * 128, kpad), 1)
        hit = ((a >> 7) * LAT + (a & (LAT - 1))) == c
        sel[rows] = jnp.where(hit, 1.0, 0.0).astype(BF16)
    gmat = group_matrix(C)

    e = [jnp.int32(0)]
    for d in range(1, reach + 1):
        n = cnt_ref[jnp.maximum(k - d, 0)]
        e.append(e[-1] + jnp.where(k >= d, n, 0))
    before = e[-1]

    for d, o in pairs:
        @pl.when(k >= d)
        def _():
            copy_from(d, o).wait_recv()

    for d in range(reach + 1):
        for r in range(R):
            xf[d * R + r] = slots[d, r].astype(F32)

    W = COLS * LAT
    lane = lax.broadcasted_iota(jnp.int32, (8, W), 1)
    sub = lax.broadcasted_iota(jnp.int32, (8, W), 0)
    part = (lane >> 4) & 7
    mask = [part == ((sub + 7) & 7), part == sub, part == ((sub + 1) & 7)]
    zero128 = jnp.zeros((8, 128), F32)

    def expanded(j, r):
        if j >= 4:
            row = xf[r, j - 4 : j - 3, :]
        else:
            m = 4 - j
            d = jnp.int32(1)
            base = e[1]
            for q in range(1, reach):
                more = e[q] < m
                d = jnp.where(more, q + 1, d)
                base = jnp.where(more, e[q + 1], base)
            slot = jnp.clip(base - m, 0, SL - 1)
            row = xf[d * R + r, pl.ds(slot, 1), :]
            row = jnp.where(jnp.broadcast_to(before >= m, row.shape), row, 0.0)
        bc = jnp.broadcast_to(row, (8, W))
        prev = jnp.concatenate([zero128, bc[:, : W - 128]], axis=1)
        nxt = jnp.concatenate([bc[:, 128:], zero128], axis=1)
        ys = [
            jnp.where(mask[0], jnp.where(sub == 0, prev, bc), 0.0),
            jnp.where(mask[1], bc, 0.0),
            jnp.where(mask[2], jnp.where(sub == 7, nxt, bc), 0.0),
        ]
        return [
            jnp.concatenate([y[:, q * 128 : q * 128 + 128] for q in range(W // 128)], axis=0)
            for y in ys
        ]

    for p in range(FL // 2):
        ex = {}
        for r in range(R):
            u, v = expanded(2 * p, r), expanded(2 * p + 1, r)
            ex[r] = [jnp.concatenate([u[x], v[x]], axis=0).astype(BF16) for x in range(3)]
        for i, rows in enumerate(sets):
            lhs = jnp.concatenate([ex[r][x] for r in rows for x in range(3)], axis=1)
            gf[i, p * 2 * COLS : (p + 1) * 2 * COLS, :] = jnp.dot(
                lhs, sel[rows], preferred_element_type=F32
            )

    for c in wincopies:
        c.wait()
    MA = FA * COLS
    for r in range(R):
        i = sets.index(rows_for(r, R))
        lhs = jnp.concatenate(
            [gf[i, t * COLS : t * COLS + MA, :] for t in range(3)], axis=1
        ).astype(BF16)
        c1s[r] = jnp.dot(lhs, wpad[r], preferred_element_type=F32).astype(BF16).astype(F32)

    s1, s2 = [], []
    for f in range(FA):
        a1 = a2 = None
        for r in range(R):
            h = c1s[r, f * COLS : (f + 1) * COLS, :]
            p1 = jnp.sum(h, axis=0, keepdims=True)
            p2 = jnp.sum(h * h, axis=0, keepdims=True)
            a1 = p1 if a1 is None else a1 + p1
            a2 = p2 if a2 is None else a2 + p2
        s1.append(a1)
        s2.append(a2)
    fill = jnp.zeros((16 - 2 * FA, C), F32)
    g = group_sums(jnp.concatenate(s1 + s2 + [fill], axis=0), gmat)
    total = float(R * COLS * GW)
    mean = g[:FA] / total
    var = g[FA : 2 * FA] / total - mean * mean
    inv = lax.rsqrt(var + EPSILON)
    scale = inv * gin_ref[...]
    shift = sin_ref[...] - mean * scale

    off = 0 if R == 2 else 1
    if off:
        for z in (0, R + 1):
            la[z] = jnp.zeros(la.shape[1:], BF16)
            lb[z] = jnp.zeros(lb.shape[1:], BF16)
    for r in range(R):
        act = []
        for f in range(FA):
            u = c1s[r, f * COLS : (f + 1) * COLS, :] * scale[f : f + 1] + shift[f : f + 1]
            a = silu(u)
            if f < 2:
                a = jnp.where(jnp.broadcast_to(before >= 2 - f, a.shape), a, 0.0)
            act.append(a)
        for p in range(FA // 2):
            la[r + off, p * 2 * COLS : (p + 1) * 2 * COLS, :] = jnp.concatenate(
                act[2 * p : 2 * p + 2], axis=0
            ).astype(BF16)
        for p in range(SL // 2):
            lb[r + off, p * 2 * COLS : (p + 1) * 2 * COLS, :] = jnp.concatenate(
                act[2 * p + 1 : 2 * p + 3], axis=0
            ).astype(BF16)

    for c in wcopies:
        c.wait()
    M = SL * COLS
    first = 0 if R == 2 else b
    lhs = []
    for t in range(3):
        for q in range(nin):
            if t == 1:
                lhs.append(lb[first + q])
            else:
                lhs.append(la[first + q, t * COLS : t * COLS + M, :])
    lhs = jnp.concatenate(lhs, axis=1)
    prod = []
    for x in range(3):
        rhs = jnp.concatenate([wv[t, q, x] for t in range(3) for q in range(nin)], axis=1)
        prod.append(
            lax.dot_general(
                lhs, rhs, (((1,), (1,)), ((), ())), preferred_element_type=F32
            )
        )
    hs, t1, t2 = [], [], []
    col = lax.broadcasted_iota(jnp.int32, (COLS, half), 0)
    for f in range(SL):
        p0, p1, p2 = [p[f * COLS : (f + 1) * COLS] for p in prod]
        h = p1 + jnp.where(col == 0, 0.0, pltpu.roll(p0, 1, 0))
        h = h + jnp.where(col == COLS - 1, 0.0, pltpu.roll(p2, COLS - 1, 0))
        h = h.astype(BF16).astype(F32)
        hs.append(h)
        t1.append(jnp.sum(h, axis=0, keepdims=True))
        t2.append(jnp.sum(h * h, axis=0, keepdims=True))
    stats[b] = jnp.concatenate(t1 + t2, axis=0)

    def stat_copy(o, place):
        return pltpu.make_async_remote_copy(
            src_ref=stats.at[place],
            dst_ref=stats.at[place],
            send_sem=st_send.at[o],
            recv_sem=st_recv.at[o],
            device_id={"band": lax.rem(b + o, R)},
            device_id_type=MESH,
        )

    for o in range(1, R):
        stat_copy(o, b).start()
    gmat2 = group_matrix(half)
    for o in range(1, R):
        stat_copy(o, lax.rem(b + R - o, R)).wait_recv()
    both = stats[0]
    for r in range(1, R):
        both = both + stats[r]
    pad = jnp.zeros((16 - 2 * SL, half), F32)
    g = group_sums(jnp.concatenate([both, pad], axis=0), gmat2)
    mean = g[:SL] / total
    var = g[SL : 2 * SL] / total - mean * mean
    inv = lax.rsqrt(var + EPSILON)
    scale = inv * gout_ref[...]
    shift = sout_ref[...] - mean * scale
    for f in range(SL):
        a = silu(hs[f] * scale[f : f + 1] + shift[f : f + 1])
        out_ref[f] = a.T.astype(BF16)

    for d, o in pairs:
        @pl.when(k + d < nb)
        def _():
            copy_to(d, o).wait_send()
    for o in range(1, R):
        stat_copy(o, b).wait_send()


def shards(latents, frame_counts, w_in, gain_in, shift_in, w_mid, gain_out, shift_out):
    SL, band_rows, width = latents.shape
    COLS = width // LAT
    half = w_mid.shape[4]
    R = lax.axis_size("band") * band_rows
    nb = lax.axis_size("block")
    reach = min(4, nb - 1)
    nin = min(3, R)
    FL, FA = SL + 4, SL + 2
    sets = set(rows_for(r, R) for r in range(R))
    kpad = up(max(len(s) for s in sets) * 3 * LAT, 128)
    extra = 0 if R == 2 else 2
    vmem = pl.BlockSpec(memory_space=pltpu.VMEM)
    hbm = pl.BlockSpec(memory_space=pl.ANY)
    raw = pl.pallas_call(
        functools.partial(body, nb, R, COLS, SL, reach),
        out_shape=jax.ShapeDtypeStruct((SL, half, COLS), BF16),
        in_specs=[
            pl.BlockSpec(memory_space=pltpu.SMEM), vmem, hbm, vmem, vmem, hbm, vmem, vmem,
        ],
        out_specs=vmem,
        scratch_shapes=[
            pltpu.VMEM((reach + 1, R, SL, width), BF16),
            pltpu.VMEM(((reach + 1) * R, SL, width), F32),
            pltpu.VMEM((len(sets), FL * COLS, kpad), F32),
            pltpu.VMEM((R, 3 * kpad, C), BF16),
            pltpu.VMEM((R, FA * COLS, C), F32),
            pltpu.VMEM((R + extra, FA * COLS, C), BF16),
            pltpu.VMEM((R + extra, SL * COLS, C), BF16),
            pltpu.VMEM((3, nin, 3, half, C), BF16),
            pltpu.VMEM((R, 2 * SL, half), F32),
            pltpu.SemaphoreType.DMA((reach + 1, R)),
            pltpu.SemaphoreType.DMA((reach + 1, R)),
            pltpu.SemaphoreType.DMA((R,)),
            pltpu.SemaphoreType.DMA((R,)),
            pltpu.SemaphoreType.DMA((3,)),
            pltpu.SemaphoreType.DMA((R, 3)),
        ],
        compiler_params=pltpu.CompilerParams(
            collective_id=0, has_side_effects=True, vmem_limit_bytes=56 * 1024 * 1024
        ),
    )(
        frame_counts,
        latents.reshape(SL, width),
        w_in.reshape(3, 9 * LAT, C),
        gain_in.reshape(1, C),
        shift_in.reshape(1, C),
        jnp.swapaxes(w_mid, 3, 4),
        gain_out.reshape(1, half),
        shift_out.reshape(1, half),
    )
    position = lax.axis_index("block")
    live = jnp.sum(jnp.where(jnp.arange(nb, dtype=jnp.int32) == position, frame_counts, 0))
    alive = jnp.arange(SL, dtype=jnp.int32) < live
    out = jnp.where(alive[:, None, None], raw, jnp.zeros_like(raw))
    return jnp.swapaxes(out, 1, 2)[:, None]


def solution(mesh):
    return jax.shard_map(
        shards,
        mesh=mesh,
        in_specs=(
            P(("video", "block"), "band", None),
            P("video"),
            P(),
            P(),
            P(),
            P(None, None, None, None, "chan"),
            P("chan"),
            P("chan"),
        ),
        out_specs=P(("video", "block"), "band", None, "chan"),
        check_vma=False,
    )
```

```python
import functools

import jax
import jax.numpy as jnp
from jax import lax
from jax.experimental import pallas as pl
from jax.experimental.pallas import tpu as pltpu
from jax.sharding import PartitionSpec as P

LAT = 16
C = 384
GROUPS = 32
GW = C // GROUPS
EPSILON = 1e-06
MESH = pl.DeviceIdType.MESH
F32 = jnp.float32
BF16 = jnp.bfloat16


def up(n, m):
    return (n + m - 1) // m * m


def rows_for(r, R):
    return tuple(range(max(0, r - 1), min(R - 1, r + 1) + 1))


def group_matrix(n):
    a = lax.broadcasted_iota(jnp.int32, (n, n), 0)
    b = lax.broadcasted_iota(jnp.int32, (n, n), 1)
    same = ((a * 5462) >> 16) == ((b * 5462) >> 16)
    return jnp.where(same, 1.0, 0.0).astype(BF16)


def group_sums(x, gmat):
    hi = x.astype(BF16)
    rest = x - hi.astype(F32)
    mid = rest.astype(BF16)
    lo = (rest - mid.astype(F32)).astype(BF16)
    n = x.shape[0]
    y = jnp.dot(
        jnp.concatenate([hi, mid, lo], axis=0), gmat, preferred_element_type=F32
    )
    return y[:n] + y[n : 2 * n] + y[2 * n :]


def silu_twice(v):
    return v + v * jnp.tanh(v)


def body(
    nb, R, COLS, SL, reach,
    cnt_hbm, lat_ref, win_ref, gin_hbm, sin_hbm, wmid_ref, gout_hbm, sout_hbm,
    out_ref,
    cnt_ref, gin_ref, sin_ref, gout_ref, sout_ref,
    slots, xf, gf, wpad, c1s, la, lb, wv, stats,
    send_sem, recv_sem, st_send, st_recv, w_sem, win_sem, in_sem,
):
    k = lax.axis_index("block")
    b = lax.axis_index("band")
    half = out_ref.shape[1]
    FL = SL + 4
    FA = SL + 2
    nin = min(3, R)
    sets = sorted(set(rows_for(r, R) for r in range(R)))

    y0 = 1 - b if R == 2 else 0
    wcopies = []
    for t in range(3):
        c = pltpu.make_async_copy(
            wmid_ref.at[t, pl.ds(y0, nin)], wv.at[t], w_sem.at[t]
        )
        wcopies.append(c)
    wincopies = []
    kpad = wpad.shape[1] // 3
    for r in range(R):
        rows = rows_for(r, R)
        first = (rows[0] - r + 1) * 3 * LAT
        size = len(rows) * 3 * LAT
        for t in range(3):
            c = pltpu.make_async_copy(
                win_ref.at[t, pl.ds(first, size)],
                wpad.at[r, pl.ds(t * kpad, size)],
                win_sem.at[r, t],
            )
            wincopies.append(c)
    barrier = pltpu.get_barrier_semaphore()
    pairs = [(d, o) for d in range(reach + 1) for o in range(R) if (d, o) != (0, 0)]
    for d, o in pairs:
        @pl.when(k >= d)
        def _():
            pl.semaphore_signal(
                barrier, inc=1,
                device_id={"block": k - d, "band": lax.rem(b + R - o, R)},
                device_id_type=MESH,
            )
    small = [
        pltpu.make_async_copy(src, dst, in_sem.at[i])
        for i, (src, dst) in enumerate(
            [
                (lat_ref, slots.at[0, b]), (cnt_hbm, cnt_ref), (gin_hbm, gin_ref),
                (sin_hbm, sin_ref), (gout_hbm, gout_ref), (sout_hbm, sout_ref),
            ]
        )
    ]
    for c in small + wincopies + wcopies:
        c.start()
    for r in range(R):
        size = len(rows_for(r, R)) * 3 * LAT
        if size < kpad:
            for t in range(3):
                wpad[r, t * kpad + size : (t + 1) * kpad, :] = jnp.zeros((kpad - size, C), BF16)
    pl.semaphore_wait(barrier, jnp.minimum(reach + 1, nb - k) * R - 1)

    def copy_to(d, o):
        return pltpu.make_async_remote_copy(
            src_ref=lat_ref,
            dst_ref=slots.at[d, b],
            send_sem=send_sem.at[d, o],
            recv_sem=recv_sem.at[d, o],
            device_id={"block": k + d, "band": lax.rem(b + o, R)},
            device_id_type=MESH,
        )

    def copy_from(d, o):
        return pltpu.make_async_remote_copy(
            src_ref=lat_ref,
            dst_ref=slots.at[d, lax.rem(b + R - o, R)],
            send_sem=send_sem.at[d, o],
            recv_sem=recv_sem.at[d, o],
            device_id={"block": k, "band": lax.rem(b + o, R)},
            device_id_type=MESH,
        )

    for d, o in reversed(pairs):
        @pl.when(k + d < nb)
        def _():
            copy_to(d, o).start()

    sel = {}
    for rows in sets:
        n = len(rows)
        a = lax.broadcasted_iota(jnp.int32, (n * 3 * 128, kpad), 0)
        c = lax.broadcasted_iota(jnp.int32, (n * 3 * 128, kpad), 1)
        hit = ((a >> 7) * LAT + (a & (LAT - 1))) == c
        sel[rows] = jnp.where(hit, 1.0, 0.0).astype(BF16)
    gmat = group_matrix(C)

    small[1].wait()
    e = [jnp.int32(0)]
    for d in range(1, reach + 1):
        n = cnt_ref[jnp.maximum(k - d, 0)]
        e.append(e[-1] + jnp.where(k >= d, n, 0))
    before = e[-1]
    live = cnt_ref[k]

    def arrived(some):
        for d, o in pairs:
            if d in some:
                @pl.when(k >= d)
                def _():
                    copy_from(d, o).wait_recv()
        for d in some:
            for r in range(R):
                xf[d * R + r] = slots[d, r].astype(F32)

    small[0].wait()
    arrived((0,))
    W = COLS * LAT
    lane = lax.broadcasted_iota(jnp.int32, (8, W), 1)
    sub = lax.broadcasted_iota(jnp.int32, (8, W), 0)
    part = (lane >> 4) & 7
    mask = [part == ((sub + 7) & 7), part == sub, part == ((sub + 1) & 7)]
    zero128 = jnp.zeros((8, 128), F32)

    def expanded(j, r):
        if j >= 4:
            row = xf[r, j - 4 : j - 3, :]
        else:
            m = 4 - j
            d = jnp.int32(1)
            base = e[1]
            for q in range(1, reach):
                more = e[q] < m
                d = jnp.where(more, q + 1, d)
                base = jnp.where(more, e[q + 1], base)
            slot = jnp.clip(base - m, 0, SL - 1)
            row = xf[d * R + r, pl.ds(slot, 1), :]
            row = jnp.where(jnp.broadcast_to(before >= m, row.shape), row, 0.0)
        bc = jnp.broadcast_to(row, (8, W))
        prev = jnp.concatenate([zero128, bc[:, : W - 128]], axis=1)
        nxt = jnp.concatenate([bc[:, 128:], zero128], axis=1)
        ys = [
            jnp.where(mask[0], jnp.where(sub == 0, prev, bc), 0.0),
            jnp.where(mask[1], bc, 0.0),
            jnp.where(mask[2], jnp.where(sub == 7, nxt, bc), 0.0),
        ]
        return [
            jnp.concatenate([y[:, q * 128 : q * 128 + 128] for q in range(W // 128)], axis=0)
            for y in ys
        ]

    for p in reversed(range(FL // 2)):
        if p == 1:
            arrived(range(1, reach + 1))
        ex = {}
        for r in range(R):
            u, v = expanded(2 * p, r), expanded(2 * p + 1, r)
            ex[r] = [jnp.concatenate([u[x], v[x]], axis=0).astype(BF16) for x in range(3)]
        for i, rows in enumerate(sets):
            lhs = jnp.concatenate([ex[r][x] for r in rows for x in range(3)], axis=1)
            gf[i, p * 2 * COLS : (p + 1) * 2 * COLS, :] = jnp.dot(
                lhs, sel[rows], preferred_element_type=F32
            )

    for c in wincopies:
        c.wait()
    MA = FA * COLS
    for i, rows in enumerate(sets):
        mine = [r for r in range(R) if rows_for(r, R) == rows]
        lhs = jnp.concatenate(
            [gf[i, t * COLS : t * COLS + MA, :] for t in range(3)], axis=1
        ).astype(BF16)
        rhs = jnp.concatenate([wpad[r] for r in mine], axis=1)
        y = jnp.dot(lhs, rhs, preferred_element_type=F32).astype(BF16).astype(F32)
        for at, r in enumerate(mine):
            c1s[r] = y[:, at * C : (at + 1) * C]

    s1, s2 = [], []
    for f in range(FA):
        a1 = a2 = None
        for r in range(R):
            h = c1s[r, f * COLS : (f + 1) * COLS, :]
            p1 = jnp.sum(h, axis=0, keepdims=True)
            p2 = jnp.sum(h * h, axis=0, keepdims=True)
            a1 = p1 if a1 is None else a1 + p1
            a2 = p2 if a2 is None else a2 + p2
        s1.append(a1)
        s2.append(a2)
    fill = jnp.zeros((16 - 2 * FA, C), F32)
    g = group_sums(jnp.concatenate(s1 + s2 + [fill], axis=0), gmat)
    total = float(R * COLS * GW)
    mean = g[:FA] / total
    var = g[FA : 2 * FA] / total - mean * mean
    inv = lax.rsqrt(var + EPSILON)
    for c in small[2:]:
        c.wait()
    scale = inv * (0.5 * gin_ref[...].reshape(1, C))
    shift = 0.5 * sin_ref[...].reshape(1, C) - mean * scale

    off = 0 if R == 2 else 1
    if off:
        for z in (0, R + 1):
            la[z] = jnp.zeros(la.shape[1:], BF16)
            lb[z] = jnp.zeros(lb.shape[1:], BF16)
    for r in range(R):
        act = []
        for f in range(FA):
            u = c1s[r, f * COLS : (f + 1) * COLS, :] * scale[f : f + 1] + shift[f : f + 1]
            a = silu_twice(u)
            if f < 2:
                a = jnp.where(jnp.broadcast_to(before >= 2 - f, a.shape), a, 0.0)
            act.append(a)
        for p in range(FA // 2):
            la[r + off, p * 2 * COLS : (p + 1) * 2 * COLS, :] = jnp.concatenate(
                act[2 * p : 2 * p + 2], axis=0
            ).astype(BF16)
        for p in range(SL // 2):
            lb[r + off, p * 2 * COLS : (p + 1) * 2 * COLS, :] = jnp.concatenate(
                act[2 * p + 1 : 2 * p + 3], axis=0
            ).astype(BF16)

    for c in wcopies:
        c.wait()
    M = SL * COLS
    first = 0 if R == 2 else b
    lhs = []
    for t in range(3):
        for q in range(nin):
            if t == 1:
                lhs.append(lb[first + q])
            else:
                lhs.append(la[first + q, t * COLS : t * COLS + M, :])
    lhs = jnp.concatenate(lhs, axis=1)
    prod = []
    for x in range(3):
        rhs = jnp.concatenate([wv[t, q, x] for t in range(3) for q in range(nin)], axis=1)
        prod.append(
            lax.dot_general(
                lhs, rhs, (((1,), (1,)), ((), ())), preferred_element_type=F32
            )
        )
    hs, t1, t2 = [], [], []
    col = lax.broadcasted_iota(jnp.int32, (COLS, half), 0)
    for f in range(SL):
        p0, p1, p2 = [p[f * COLS : (f + 1) * COLS] for p in prod]
        h = p1 + jnp.where(col == 0, 0.0, pltpu.roll(p0, 1, 0))
        h = h + jnp.where(col == COLS - 1, 0.0, pltpu.roll(p2, COLS - 1, 0))
        h = h.astype(BF16).astype(F32)
        hs.append(h)
        t1.append(jnp.sum(h, axis=0, keepdims=True))
        t2.append(jnp.sum(h * h, axis=0, keepdims=True))
    stats[b] = jnp.concatenate(t1 + t2, axis=0)

    def stat_copy(o, place):
        return pltpu.make_async_remote_copy(
            src_ref=stats.at[place],
            dst_ref=stats.at[place],
            send_sem=st_send.at[o],
            recv_sem=st_recv.at[o],
            device_id={"band": lax.rem(b + o, R)},
            device_id_type=MESH,
        )

    for o in range(1, R):
        stat_copy(o, b).start()
    gmat2 = group_matrix(half)
    for o in range(1, R):
        stat_copy(o, lax.rem(b + R - o, R)).wait_recv()
    both = stats[0]
    for r in range(1, R):
        both = both + stats[r]
    pad = jnp.zeros((16 - 2 * SL, half), F32)
    g = group_sums(jnp.concatenate([both, pad], axis=0), gmat2)
    mean = g[:SL] / total
    var = g[SL : 2 * SL] / total - mean * mean
    inv = lax.rsqrt(var + EPSILON)
    scale = inv * (0.5 * gout_ref[...].reshape(1, half))
    shift = 0.5 * sout_ref[...].reshape(1, half) - mean * scale
    for f in range(SL):
        a = silu_twice(hs[f] * scale[f : f + 1] + shift[f : f + 1])
        a = jnp.where(jnp.broadcast_to(f < live, a.shape), a, 0.0)
        out_ref[f] = a.T.astype(BF16)

    for d, o in pairs:
        @pl.when(k + d < nb)
        def _():
            copy_to(d, o).wait_send()
    for o in range(1, R):
        stat_copy(o, b).wait_send()


def shards(latents, frame_counts, w_in, gain_in, shift_in, w_mid, gain_out, shift_out):
    SL, band_rows, width = latents.shape
    COLS = width // LAT
    half = w_mid.shape[4]
    R = lax.axis_size("band") * band_rows
    nb = lax.axis_size("block")
    reach = min(4, nb - 1)
    nin = min(3, R)
    FL, FA = SL + 4, SL + 2
    sets = set(rows_for(r, R) for r in range(R))
    kpad = up(max(len(s) for s in sets) * 3 * LAT, 128)
    extra = 0 if R == 2 else 2
    vmem = pl.BlockSpec(memory_space=pltpu.VMEM)
    hbm = pl.BlockSpec(memory_space=pltpu.HBM)
    raw = pl.pallas_call(
        functools.partial(body, nb, R, COLS, SL, reach),
        out_shape=jax.ShapeDtypeStruct((SL, half, COLS), BF16),
        in_specs=[hbm] * 8,
        out_specs=vmem,
        scratch_shapes=[
            pltpu.SMEM(frame_counts.shape, jnp.int32),
            pltpu.VMEM((C,), F32),
            pltpu.VMEM((C,), F32),
            pltpu.VMEM((half,), F32),
            pltpu.VMEM((half,), F32),
            pltpu.VMEM((reach + 1, R, SL, width), BF16),
            pltpu.VMEM(((reach + 1) * R, SL, width), F32),
            pltpu.VMEM((len(sets), FL * COLS, kpad), F32),
            pltpu.VMEM((R, 3 * kpad, C), BF16),
            pltpu.VMEM((R, FA * COLS, C), F32),
            pltpu.VMEM((R + extra, FA * COLS, C), BF16),
            pltpu.VMEM((R + extra, SL * COLS, C), BF16),
            pltpu.VMEM((3, nin, 3, half, C), BF16),
            pltpu.VMEM((R, 2 * SL, half), F32),
            pltpu.SemaphoreType.DMA((reach + 1, R)),
            pltpu.SemaphoreType.DMA((reach + 1, R)),
            pltpu.SemaphoreType.DMA((R,)),
            pltpu.SemaphoreType.DMA((R,)),
            pltpu.SemaphoreType.DMA((3,)),
            pltpu.SemaphoreType.DMA((R, 3)),
            pltpu.SemaphoreType.DMA((6,)),
        ],
        compiler_params=pltpu.CompilerParams(
            collective_id=0, has_side_effects=True, vmem_limit_bytes=24 * 1024 * 1024
        ),
    )(
        frame_counts,
        latents.reshape(SL, width),
        w_in.reshape(3, 9 * LAT, C),
        gain_in,
        shift_in,
        jnp.swapaxes(w_mid, 3, 4),
        gain_out,
        shift_out,
    )
    return jnp.swapaxes(raw, 1, 2)[:, None]


def solution(mesh):
    return jax.shard_map(
        shards,
        mesh=mesh,
        in_specs=(
            P(("video", "block"), "band", None),
            P("video"),
            P(),
            P(),
            P(),
            P(None, None, None, None, "chan"),
            P("chan"),
            P("chan"),
        ),
        out_specs=P(("video", "block"), "band", None, "chan"),
        check_vma=False,
    )
```

```python
import functools

import jax
import jax.numpy as jnp
from jax import lax
from jax.experimental import pallas as pl
from jax.experimental.pallas import tpu as pltpu
from jax.sharding import PartitionSpec as P

LAT = 16
C = 384
GROUPS = 32
GW = C // GROUPS
EPSILON = 1e-06
MESH = pl.DeviceIdType.MESH
F32 = jnp.float32
BF16 = jnp.bfloat16


def up(n, m):
    return (n + m - 1) // m * m


def rows_for(r, R):
    return tuple(range(max(0, r - 1), min(R - 1, r + 1) + 1))


def group_matrix(n):
    a = lax.broadcasted_iota(jnp.int32, (n, n), 0)
    b = lax.broadcasted_iota(jnp.int32, (n, n), 1)
    same = ((a * 5462) >> 16) == ((b * 5462) >> 16)
    return jnp.where(same, 1.0, 0.0).astype(BF16)


def group_sums(x, gmat):
    hi = x.astype(BF16)
    rest = x - hi.astype(F32)
    mid = rest.astype(BF16)
    lo = (rest - mid.astype(F32)).astype(BF16)
    n = x.shape[0]
    y = jnp.dot(
        jnp.concatenate([hi, mid, lo], axis=0), gmat, preferred_element_type=F32
    )
    return y[:n] + y[n : 2 * n] + y[2 * n :]


def silu_twice(v):
    return v + v * jnp.tanh(v)


def body(
    nb, R, COLS, SL, reach,
    cnt_hbm, lat_ref, win_ref, gin_hbm, sin_hbm, wmid_ref, gout_hbm, sout_hbm,
    out_ref,
    cnt_ref, gin_ref, sin_ref, gout_ref, sout_ref,
    slots, xf, gf, wpad, c1s, la, lb, wv, stats,
    send_sem, recv_sem, st_send, st_recv, w_sem, win_sem, in_sem,
):
    k = lax.axis_index("block")
    b = lax.axis_index("band")
    half = out_ref.shape[1]
    FL = SL + 4
    FA = SL + 2
    nin = min(3, R)
    sets = sorted(set(rows_for(r, R) for r in range(R)))

    y0 = 1 - b if R == 2 else 0
    wcopies = []
    for t in range(3):
        c = pltpu.make_async_copy(
            wmid_ref.at[t, pl.ds(y0, nin)], wv.at[t], w_sem.at[t]
        )
        wcopies.append(c)
    wincopies = []
    kpad = wpad.shape[1] // 3
    for r in range(R):
        rows = rows_for(r, R)
        first = (rows[0] - r + 1) * 3 * LAT
        size = len(rows) * 3 * LAT
        for t in range(3):
            c = pltpu.make_async_copy(
                win_ref.at[t, pl.ds(first, size)],
                wpad.at[r, pl.ds(t * kpad, size)],
                win_sem.at[r, t],
            )
            wincopies.append(c)
    barrier = pltpu.get_barrier_semaphore()
    pairs = [(d, o) for d in range(reach + 1) for o in range(R) if (d, o) != (0, 0)]
    for d, o in pairs:
        @pl.when(k >= d)
        def _():
            pl.semaphore_signal(
                barrier, inc=1,
                device_id={"block": k - d, "band": lax.rem(b + R - o, R)},
                device_id_type=MESH,
            )
    small = [
        pltpu.make_async_copy(src, dst, in_sem.at[i])
        for i, (src, dst) in enumerate(
            [
                (lat_ref, slots.at[0, b]), (cnt_hbm, cnt_ref), (gin_hbm, gin_ref),
                (sin_hbm, sin_ref), (gout_hbm, gout_ref), (sout_hbm, sout_ref),
            ]
        )
    ]
    for c in small + wincopies + wcopies:
        c.start()
    for r in range(R):
        size = len(rows_for(r, R)) * 3 * LAT
        if size < kpad:
            for t in range(3):
                wpad[r, t * kpad + size : (t + 1) * kpad, :] = jnp.zeros((kpad - size, C), BF16)
    pl.semaphore_wait(barrier, jnp.minimum(reach + 1, nb - k) * R - 1)

    def copy_to(d, o):
        return pltpu.make_async_remote_copy(
            src_ref=lat_ref,
            dst_ref=slots.at[d, b],
            send_sem=send_sem.at[d, o],
            recv_sem=recv_sem.at[d, o],
            device_id={"block": k + d, "band": lax.rem(b + o, R)},
            device_id_type=MESH,
        )

    def copy_from(d, o):
        return pltpu.make_async_remote_copy(
            src_ref=lat_ref,
            dst_ref=slots.at[d, lax.rem(b + R - o, R)],
            send_sem=send_sem.at[d, o],
            recv_sem=recv_sem.at[d, o],
            device_id={"block": k, "band": lax.rem(b + o, R)},
            device_id_type=MESH,
        )

    for d, o in reversed(pairs):
        @pl.when(k + d < nb)
        def _():
            copy_to(d, o).start()

    sel = {}
    for rows in sets:
        n = len(rows)
        a = lax.broadcasted_iota(jnp.int32, (n * 3 * 128, kpad), 0)
        c = lax.broadcasted_iota(jnp.int32, (n * 3 * 128, kpad), 1)
        hit = ((a >> 7) * LAT + (a & (LAT - 1))) == c
        sel[rows] = jnp.where(hit, 1.0, 0.0).astype(BF16)
    gmat = group_matrix(C)

    small[1].wait()
    e = [jnp.int32(0)]
    for d in range(1, reach + 1):
        n = cnt_ref[jnp.maximum(k - d, 0)]
        e.append(e[-1] + jnp.where(k >= d, n, 0))
    before = e[-1]
    live = cnt_ref[k]

    def arrived(some):
        for d, o in pairs:
            if d in some:
                @pl.when(k >= d)
                def _():
                    copy_from(d, o).wait_recv()
        for d in some:
            for r in range(R):
                xf[d * R + r] = slots[d, r].astype(F32)

    small[0].wait()
    arrived((0,))
    W = COLS * LAT
    lane = lax.broadcasted_iota(jnp.int32, (8, W), 1)
    sub = lax.broadcasted_iota(jnp.int32, (8, W), 0)
    part = (lane >> 4) & 7
    mask = [part == ((sub + 7) & 7), part == sub, part == ((sub + 1) & 7)]
    zero128 = jnp.zeros((8, 128), F32)

    def expanded(j, r):
        if j >= 4:
            row = xf[r, j - 4 : j - 3, :]
        else:
            m = 4 - j
            d = jnp.int32(1)
            base = e[1]
            for q in range(1, reach):
                more = e[q] < m
                d = jnp.where(more, q + 1, d)
                base = jnp.where(more, e[q + 1], base)
            slot = jnp.clip(base - m, 0, SL - 1)
            row = xf[d * R + r, pl.ds(slot, 1), :]
            row = jnp.where(jnp.broadcast_to(before >= m, row.shape), row, 0.0)
        bc = jnp.broadcast_to(row, (8, W))
        prev = jnp.concatenate([zero128, bc[:, : W - 128]], axis=1)
        nxt = jnp.concatenate([bc[:, 128:], zero128], axis=1)
        ys = [
            jnp.where(mask[0], jnp.where(sub == 0, prev, bc), 0.0),
            jnp.where(mask[1], bc, 0.0),
            jnp.where(mask[2], jnp.where(sub == 7, nxt, bc), 0.0),
        ]
        return [
            jnp.concatenate([y[:, q * 128 : q * 128 + 128] for q in range(W // 128)], axis=0)
            for y in ys
        ]

    for p in reversed(range(FL // 2)):
        if p == 1:
            arrived(range(1, reach + 1))
        ex = {}
        for r in range(R):
            u, v = expanded(2 * p, r), expanded(2 * p + 1, r)
            ex[r] = [jnp.concatenate([u[x], v[x]], axis=0).astype(BF16) for x in range(3)]
        for i, rows in enumerate(sets):
            lhs = jnp.concatenate([ex[r][x] for r in rows for x in range(3)], axis=1)
            gf[i, p * 2 * COLS : (p + 1) * 2 * COLS, :] = jnp.dot(
                lhs, sel[rows], preferred_element_type=F32
            )

    for c in wincopies:
        c.wait()
    MA = FA * COLS
    for i, rows in enumerate(sets):
        mine = [r for r in range(R) if rows_for(r, R) == rows]
        lhs = jnp.concatenate(
            [gf[i, t * COLS : t * COLS + MA, :] for t in range(3)], axis=1
        ).astype(BF16)
        rhs = jnp.concatenate([wpad[r] for r in mine], axis=1)
        y = jnp.dot(lhs, rhs, preferred_element_type=F32).astype(BF16).astype(F32)
        for at, r in enumerate(mine):
            c1s[r] = y[:, at * C : (at + 1) * C]

    s1, s2 = [], []
    for f in range(FA):
        a1 = a2 = None
        for r in range(R):
            h = c1s[r, f * COLS : (f + 1) * COLS, :]
            p1 = jnp.sum(h, axis=0, keepdims=True)
            p2 = jnp.sum(h * h, axis=0, keepdims=True)
            a1 = p1 if a1 is None else a1 + p1
            a2 = p2 if a2 is None else a2 + p2
        s1.append(a1)
        s2.append(a2)
    fill = jnp.zeros((16 - 2 * FA, C), F32)
    g = group_sums(jnp.concatenate(s1 + s2 + [fill], axis=0), gmat)
    total = float(R * COLS * GW)
    mean = g[:FA] / total
    var = g[FA : 2 * FA] / total - mean * mean
    inv = lax.rsqrt(var + EPSILON)
    for c in small[2:]:
        c.wait()
    scale = inv * (0.5 * gin_ref[...].reshape(1, C))
    shift = 0.5 * sin_ref[...].reshape(1, C) - mean * scale

    off = 0 if R == 2 else 1
    if off:
        for z in (0, R + 1):
            la[z] = jnp.zeros(la.shape[1:], BF16)
            lb[z] = jnp.zeros(lb.shape[1:], BF16)
    for r in range(R):
        act = []
        for f in range(FA):
            u = c1s[r, f * COLS : (f + 1) * COLS, :] * scale[f : f + 1] + shift[f : f + 1]
            a = silu_twice(u)
            if f < 2:
                a = jnp.where(jnp.broadcast_to(before >= 2 - f, a.shape), a, 0.0)
            act.append(a)
        for p in range(FA // 2):
            la[r + off, p * 2 * COLS : (p + 1) * 2 * COLS, :] = jnp.concatenate(
                act[2 * p : 2 * p + 2], axis=0
            ).astype(BF16)
        for p in range(SL // 2):
            lb[r + off, p * 2 * COLS : (p + 1) * 2 * COLS, :] = jnp.concatenate(
                act[2 * p + 1 : 2 * p + 3], axis=0
            ).astype(BF16)

    for c in wcopies:
        c.wait()
    M = SL * COLS
    first = 0 if R == 2 else b
    lhs = []
    for t in range(3):
        for q in range(nin):
            if t == 1:
                lhs.append(lb[first + q])
            else:
                lhs.append(la[first + q, t * COLS : t * COLS + M, :])
    lhs = jnp.concatenate(lhs, axis=1)
    prod = []
    for x in range(3):
        rhs = jnp.concatenate([wv[t, q, x] for t in range(3) for q in range(nin)], axis=1)
        prod.append(
            lax.dot_general(
                lhs, rhs, (((1,), (1,)), ((), ())), preferred_element_type=F32
            )
        )
    hs, t1, t2 = [], [], []
    col = lax.broadcasted_iota(jnp.int32, (COLS, half), 0)
    for f in range(SL):
        p0, p1, p2 = [p[f * COLS : (f + 1) * COLS] for p in prod]
        h = p1 + jnp.where(col == 0, 0.0, pltpu.roll(p0, 1, 0))
        h = h + jnp.where(col == COLS - 1, 0.0, pltpu.roll(p2, COLS - 1, 0))
        h = h.astype(BF16).astype(F32)
        hs.append(h)
        t1.append(jnp.sum(h, axis=0, keepdims=True))
        t2.append(jnp.sum(h * h, axis=0, keepdims=True))
    stats[b] = jnp.concatenate(t1 + t2, axis=0)

    def stat_copy(o, place):
        return pltpu.make_async_remote_copy(
            src_ref=stats.at[place],
            dst_ref=stats.at[place],
            send_sem=st_send.at[o],
            recv_sem=st_recv.at[o],
            device_id={"band": lax.rem(b + o, R)},
            device_id_type=MESH,
        )

    for o in range(1, R):
        stat_copy(o, b).start()
    gmat2 = group_matrix(half)
    for o in range(1, R):
        stat_copy(o, lax.rem(b + R - o, R)).wait_recv()
    both = stats[0]
    for r in range(1, R):
        both = both + stats[r]
    pad = jnp.zeros((16 - 2 * SL, half), F32)
    g = group_sums(jnp.concatenate([both, pad], axis=0), gmat2)
    mean = g[:SL] / total
    var = g[SL : 2 * SL] / total - mean * mean
    inv = lax.rsqrt(var + EPSILON)
    scale = inv * (0.5 * gout_ref[...].reshape(1, half))
    shift = 0.5 * sout_ref[...].reshape(1, half) - mean * scale
    for f in range(SL):
        a = silu_twice(hs[f] * scale[f : f + 1] + shift[f : f + 1])
        a = jnp.where(jnp.broadcast_to(f < live, a.shape), a, 0.0)
        out_ref[f] = a.T.astype(BF16)

    for d, o in pairs:
        @pl.when(k + d < nb)
        def _():
            copy_to(d, o).wait_send()
    for o in range(1, R):
        stat_copy(o, b).wait_send()


def shards(latents, frame_counts, w_in, gain_in, shift_in, w_mid, gain_out, shift_out):
    SL, band_rows, width = latents.shape
    COLS = width // LAT
    half = w_mid.shape[4]
    R = lax.axis_size("band") * band_rows
    nb = lax.axis_size("block")
    reach = min(4, nb - 1)
    nin = min(3, R)
    FL, FA = SL + 4, SL + 2
    sets = set(rows_for(r, R) for r in range(R))
    kpad = up(max(len(s) for s in sets) * 3 * LAT, 128)
    extra = 0 if R == 2 else 2
    vmem = pl.BlockSpec(memory_space=pltpu.VMEM)
    hbm = pl.BlockSpec(memory_space=pltpu.HBM)
    raw = pl.pallas_call(
        functools.partial(body, nb, R, COLS, SL, reach),
        out_shape=pltpu.VMEM((SL, half, COLS), BF16),
        in_specs=[hbm] * 8,
        out_specs=vmem,
        scratch_shapes=[
            pltpu.SMEM(frame_counts.shape, jnp.int32),
            pltpu.VMEM((C,), F32),
            pltpu.VMEM((C,), F32),
            pltpu.VMEM((half,), F32),
            pltpu.VMEM((half,), F32),
            pltpu.VMEM((reach + 1, R, SL, width), BF16),
            pltpu.VMEM(((reach + 1) * R, SL, width), F32),
            pltpu.VMEM((len(sets), FL * COLS, kpad), F32),
            pltpu.VMEM((R, 3 * kpad, C), BF16),
            pltpu.VMEM((R, FA * COLS, C), F32),
            pltpu.VMEM((R + extra, FA * COLS, C), BF16),
            pltpu.VMEM((R + extra, SL * COLS, C), BF16),
            pltpu.VMEM((3, nin, 3, half, C), BF16),
            pltpu.VMEM((R, 2 * SL, half), F32),
            pltpu.SemaphoreType.DMA((reach + 1, R)),
            pltpu.SemaphoreType.DMA((reach + 1, R)),
            pltpu.SemaphoreType.DMA((R,)),
            pltpu.SemaphoreType.DMA((R,)),
            pltpu.SemaphoreType.DMA((3,)),
            pltpu.SemaphoreType.DMA((R, 3)),
            pltpu.SemaphoreType.DMA((6,)),
        ],
        compiler_params=pltpu.CompilerParams(
            collective_id=0, has_side_effects=True, vmem_limit_bytes=40 * 1024 * 1024
        ),
    )(*[pltpu.with_memory_space_constraint(z, pltpu.HBM) for z in (
        frame_counts,
        latents.reshape(SL, width),
        w_in.reshape(3, 9 * LAT, C),
        gain_in,
        shift_in,
        jnp.swapaxes(w_mid, 3, 4),
        gain_out,
        shift_out,
    )])
    return jnp.swapaxes(raw, 1, 2)[:, None]


def solution(mesh):
    return jax.shard_map(
        shards,
        mesh=mesh,
        in_specs=(
            P(("video", "block"), "band", None),
            P("video"),
            P(),
            P(),
            P(),
            P(None, None, None, None, "chan"),
            P("chan"),
            P("chan"),
        ),
        out_specs=P(("video", "block"), "band", None, "chan"),
        check_vma=False,
    )
```

```python
import functools

import jax
import jax.numpy as jnp
from jax import lax
from jax.experimental import pallas as pl
from jax.experimental.pallas import tpu as pltpu
from jax.sharding import PartitionSpec as P

LAT = 16
C = 384
GROUPS = 32
GW = C // GROUPS
EPSILON = 1e-06
MESH = pl.DeviceIdType.MESH
F32 = jnp.float32
BF16 = jnp.bfloat16


def up(n, m):
    return (n + m - 1) // m * m


def rows_for(r, R):
    return tuple(range(max(0, r - 1), min(R - 1, r + 1) + 1))


def group_matrix(n):
    a = lax.broadcasted_iota(jnp.int32, (n, n), 0)
    b = lax.broadcasted_iota(jnp.int32, (n, n), 1)
    same = ((a * 5462) >> 16) == ((b * 5462) >> 16)
    return jnp.where(same, 1.0, 0.0).astype(BF16)


def group_sums(x, gmat):
    hi = x.astype(BF16)
    rest = x - hi.astype(F32)
    mid = rest.astype(BF16)
    lo = (rest - mid.astype(F32)).astype(BF16)
    n = x.shape[0]
    y = jnp.dot(
        jnp.concatenate([hi, mid, lo], axis=0), gmat, preferred_element_type=F32
    )
    return y[:n] + y[n : 2 * n] + y[2 * n :]


def silu_twice(v):
    return v + v * jnp.tanh(v)


def body(
    nb, R, COLS, SL, reach,
    cnt_hbm, lat_ref, win_ref, gin_hbm, sin_hbm, wmid_ref, gout_hbm, sout_hbm,
    out_ref,
    cnt_ref, gin_ref, sin_ref, gout_ref, sout_ref,
    slots, xf, gf, wpad, c1s, la, lb, wv, stats,
    send_sem, recv_sem, st_send, st_recv, w_sem, win_sem, in_sem,
):
    k = lax.axis_index("block")
    b = lax.axis_index("band")
    half = out_ref.shape[1]
    FL = SL + 4
    FA = SL + 2
    nin = min(3, R)
    sets = sorted(set(rows_for(r, R) for r in range(R)))

    y0 = 1 - b if R == 2 else 0
    wcopies = []
    for t in range(3):
        c = pltpu.make_async_copy(
            wmid_ref.at[t, pl.ds(y0, nin)], wv.at[t], w_sem.at[t]
        )
        wcopies.append(c)
    wincopies = []
    kpad = wpad.shape[1] // 3
    for r in range(R):
        rows = rows_for(r, R)
        first = (rows[0] - r + 1) * 3 * LAT
        size = len(rows) * 3 * LAT
        for t in range(3):
            c = pltpu.make_async_copy(
                win_ref.at[t, pl.ds(first, size)],
                wpad.at[r, pl.ds(t * kpad, size)],
                win_sem.at[r, t],
            )
            wincopies.append(c)
    barrier = pltpu.get_barrier_semaphore()
    near = [(d, o) for d in range(min(reach, 1) + 1) for o in range(R) if (d, o) != (0, 0)]
    for d, o in near:
        @pl.when(k >= d)
        def _():
            pl.semaphore_signal(
                barrier, inc=1,
                device_id={"block": k - d, "band": lax.rem(b + R - o, R)},
                device_id_type=MESH,
            )
    small = [
        pltpu.make_async_copy(src, dst, in_sem.at[i])
        for i, (src, dst) in enumerate(
            [
                (lat_ref, slots.at[0, b]), (cnt_hbm, cnt_ref), (gin_hbm, gin_ref),
                (sin_hbm, sin_ref), (gout_hbm, gout_ref), (sout_hbm, sout_ref),
            ]
        )
    ]
    for c in small + wincopies + wcopies:
        c.start()
    for r in range(R):
        size = len(rows_for(r, R)) * 3 * LAT
        if size < kpad:
            for t in range(3):
                wpad[r, t * kpad + size : (t + 1) * kpad, :] = jnp.zeros((kpad - size, C), BF16)

    def copy_to(d, o):
        return pltpu.make_async_remote_copy(
            src_ref=slots.at[max(d - 1, 0), b],
            dst_ref=slots.at[d, b],
            send_sem=send_sem.at[d, o],
            recv_sem=recv_sem.at[d, o],
            device_id={"block": k + min(d, 1), "band": lax.rem(b + o, R)},
            device_id_type=MESH,
        )

    def copy_from(d, o):
        return pltpu.make_async_remote_copy(
            src_ref=slots.at[max(d - 1, 0), b],
            dst_ref=slots.at[d, lax.rem(b + R - o, R)],
            send_sem=send_sem.at[d, o],
            recv_sem=recv_sem.at[d, o],
            device_id={"block": k, "band": lax.rem(b + o, R)},
            device_id_type=MESH,
        )

    def sends(d):
        return (k + 1 < nb) & (k >= d - 1)

    sel = {}
    for rows in sets:
        n = len(rows)
        a = lax.broadcasted_iota(jnp.int32, (n * 3 * 128, kpad), 0)
        c = lax.broadcasted_iota(jnp.int32, (n * 3 * 128, kpad), 1)
        hit = ((a >> 7) * LAT + (a & (LAT - 1))) == c
        sel[rows] = jnp.where(hit, 1.0, 0.0).astype(BF16)
    gmat = group_matrix(C)

    small[0].wait()
    pl.semaphore_wait(barrier, R - 1 + jnp.where(k + 1 < nb, R, 0))
    for d, o in reversed(near):
        if d == 0:
            copy_to(d, o).start()
        else:
            @pl.when(sends(d))
            def _():
                copy_to(d, o).start()
    small[1].wait()
    e = [jnp.int32(0)]
    for d in range(1, reach + 1):
        n = cnt_ref[jnp.maximum(k - d, 0)]
        e.append(e[-1] + jnp.where(k >= d, n, 0))
    before = e[-1]
    live = cnt_ref[k]

    def unpack(d):
        for r in range(R):
            xf[d * R + r] = slots[d, r].astype(F32)

    for o in range(1, R):
        copy_from(0, o).wait_recv()
    unpack(0)

    def earlier():
        for d in range(1, reach + 1):
            @pl.when(k >= d)
            def _():
                copy_from(d, 0).wait_recv()
            if d < reach:
                @pl.when(sends(d + 1))
                def _():
                    for o in range(R):
                        copy_to(d + 1, o).start()
        for d in range(1, reach + 1):
            for o in range(1, R):
                @pl.when(k >= d)
                def _():
                    copy_from(d, o).wait_recv()
            unpack(d)

    W = COLS * LAT
    lane = lax.broadcasted_iota(jnp.int32, (8, W), 1)
    sub = lax.broadcasted_iota(jnp.int32, (8, W), 0)
    part = (lane >> 4) & 7
    mask = [part == ((sub + 7) & 7), part == sub, part == ((sub + 1) & 7)]
    zero128 = jnp.zeros((8, 128), F32)

    def expanded(j, r):
        if j >= 4:
            row = xf[r, j - 4 : j - 3, :]
        else:
            m = 4 - j
            d = jnp.int32(1)
            base = e[1]
            for q in range(1, reach):
                more = e[q] < m
                d = jnp.where(more, q + 1, d)
                base = jnp.where(more, e[q + 1], base)
            slot = jnp.clip(base - m, 0, SL - 1)
            row = xf[d * R + r, pl.ds(slot, 1), :]
            row = jnp.where(jnp.broadcast_to(before >= m, row.shape), row, 0.0)
        bc = jnp.broadcast_to(row, (8, W))
        prev = jnp.concatenate([zero128, bc[:, : W - 128]], axis=1)
        nxt = jnp.concatenate([bc[:, 128:], zero128], axis=1)
        ys = [
            jnp.where(mask[0], jnp.where(sub == 0, prev, bc), 0.0),
            jnp.where(mask[1], bc, 0.0),
            jnp.where(mask[2], jnp.where(sub == 7, nxt, bc), 0.0),
        ]
        return [
            jnp.concatenate([y[:, q * 128 : q * 128 + 128] for q in range(W // 128)], axis=0)
            for y in ys
        ]

    for p in reversed(range(FL // 2)):
        if p == 1:
            earlier()
        ex = {}
        for r in range(R):
            u, v = expanded(2 * p, r), expanded(2 * p + 1, r)
            ex[r] = [jnp.concatenate([u[x], v[x]], axis=0).astype(BF16) for x in range(3)]
        for i, rows in enumerate(sets):
            lhs = jnp.concatenate([ex[r][x] for r in rows for x in range(3)], axis=1)
            gf[i, p * 2 * COLS : (p + 1) * 2 * COLS, :] = jnp.dot(
                lhs, sel[rows], preferred_element_type=F32
            )

    for c in wincopies:
        c.wait()
    MA = FA * COLS
    for i, rows in enumerate(sets):
        mine = [r for r in range(R) if rows_for(r, R) == rows]
        lhs = jnp.concatenate(
            [gf[i, t * COLS : t * COLS + MA, :] for t in range(3)], axis=1
        ).astype(BF16)
        rhs = jnp.concatenate([wpad[r] for r in mine], axis=1)
        y = jnp.dot(lhs, rhs, preferred_element_type=F32).astype(BF16).astype(F32)
        for at, r in enumerate(mine):
            c1s[r] = y[:, at * C : (at + 1) * C]

    s1, s2 = [], []
    for f in range(FA):
        a1 = a2 = None
        for r in range(R):
            h = c1s[r, f * COLS : (f + 1) * COLS, :]
            p1 = jnp.sum(h, axis=0, keepdims=True)
            p2 = jnp.sum(h * h, axis=0, keepdims=True)
            a1 = p1 if a1 is None else a1 + p1
            a2 = p2 if a2 is None else a2 + p2
        s1.append(a1)
        s2.append(a2)
    fill = jnp.zeros((16 - 2 * FA, C), F32)
    g = group_sums(jnp.concatenate(s1 + s2 + [fill], axis=0), gmat)
    total = float(R * COLS * GW)
    mean = g[:FA] / total
    var = g[FA : 2 * FA] / total - mean * mean
    inv = lax.rsqrt(var + EPSILON)
    for c in small[2:]:
        c.wait()
    scale = inv * (0.5 * gin_ref[...].reshape(1, C))
    shift = 0.5 * sin_ref[...].reshape(1, C) - mean * scale

    off = 0 if R == 2 else 1
    if off:
        for z in (0, R + 1):
            la[z] = jnp.zeros(la.shape[1:], BF16)
            lb[z] = jnp.zeros(lb.shape[1:], BF16)
    for r in range(R):
        act = []
        for f in range(FA):
            u = c1s[r, f * COLS : (f + 1) * COLS, :] * scale[f : f + 1] + shift[f : f + 1]
            a = silu_twice(u)
            if f < 2:
                a = jnp.where(jnp.broadcast_to(before >= 2 - f, a.shape), a, 0.0)
            act.append(a)
        for p in range(FA // 2):
            la[r + off, p * 2 * COLS : (p + 1) * 2 * COLS, :] = jnp.concatenate(
                act[2 * p : 2 * p + 2], axis=0
            ).astype(BF16)
        for p in range(SL // 2):
            lb[r + off, p * 2 * COLS : (p + 1) * 2 * COLS, :] = jnp.concatenate(
                act[2 * p + 1 : 2 * p + 3], axis=0
            ).astype(BF16)

    for c in wcopies:
        c.wait()
    M = SL * COLS
    first = 0 if R == 2 else b
    lhs = []
    for t in range(3):
        for q in range(nin):
            if t == 1:
                lhs.append(lb[first + q])
            else:
                lhs.append(la[first + q, t * COLS : t * COLS + M, :])
    lhs = jnp.concatenate(lhs, axis=1)
    prod = []
    for x in range(3):
        rhs = jnp.concatenate([wv[t, q, x] for t in range(3) for q in range(nin)], axis=1)
        prod.append(
            lax.dot_general(
                lhs, rhs, (((1,), (1,)), ((), ())), preferred_element_type=F32
            )
        )
    hs, t1, t2 = [], [], []
    col = lax.broadcasted_iota(jnp.int32, (COLS, half), 0)
    for f in range(SL):
        p0, p1, p2 = [p[f * COLS : (f + 1) * COLS] for p in prod]
        h = p1 + jnp.where(col == 0, 0.0, pltpu.roll(p0, 1, 0))
        h = h + jnp.where(col == COLS - 1, 0.0, pltpu.roll(p2, COLS - 1, 0))
        h = h.astype(BF16).astype(F32)
        hs.append(h)
        t1.append(jnp.sum(h, axis=0, keepdims=True))
        t2.append(jnp.sum(h * h, axis=0, keepdims=True))
    stats[b] = jnp.concatenate(t1 + t2, axis=0)

    def stat_copy(o, place):
        return pltpu.make_async_remote_copy(
            src_ref=stats.at[place],
            dst_ref=stats.at[place],
            send_sem=st_send.at[o],
            recv_sem=st_recv.at[o],
            device_id={"band": lax.rem(b + o, R)},
            device_id_type=MESH,
        )

    for o in range(1, R):
        stat_copy(o, b).start()
    gmat2 = group_matrix(half)
    for o in range(1, R):
        stat_copy(o, lax.rem(b + R - o, R)).wait_recv()
    both = stats[0]
    for r in range(1, R):
        both = both + stats[r]
    pad = jnp.zeros((16 - 2 * SL, half), F32)
    g = group_sums(jnp.concatenate([both, pad], axis=0), gmat2)
    mean = g[:SL] / total
    var = g[SL : 2 * SL] / total - mean * mean
    inv = lax.rsqrt(var + EPSILON)
    scale = inv * (0.5 * gout_ref[...].reshape(1, half))
    shift = 0.5 * sout_ref[...].reshape(1, half) - mean * scale
    for f in range(SL):
        a = silu_twice(hs[f] * scale[f : f + 1] + shift[f : f + 1])
        a = jnp.where(jnp.broadcast_to(f < live, a.shape), a, 0.0)
        out_ref[f] = a.T.astype(BF16)

    for o in range(1, R):
        copy_to(0, o).wait_send()
    for d in range(1, reach + 1):
        @pl.when(sends(d))
        def _():
            for o in range(R):
                copy_to(d, o).wait_send()
    for o in range(1, R):
        stat_copy(o, b).wait_send()


def shards(latents, frame_counts, w_in, gain_in, shift_in, w_mid, gain_out, shift_out):
    SL, band_rows, width = latents.shape
    COLS = width // LAT
    half = w_mid.shape[4]
    R = lax.axis_size("band") * band_rows
    nb = lax.axis_size("block")
    reach = min(4, nb - 1)
    nin = min(3, R)
    FL, FA = SL + 4, SL + 2
    sets = set(rows_for(r, R) for r in range(R))
    kpad = up(max(len(s) for s in sets) * 3 * LAT, 128)
    extra = 0 if R == 2 else 2
    vmem = pl.BlockSpec(memory_space=pltpu.VMEM)
    hbm = pl.BlockSpec(memory_space=pltpu.HBM)
    raw = pl.pallas_call(
        functools.partial(body, nb, R, COLS, SL, reach),
        out_shape=pltpu.VMEM((SL, half, COLS), BF16),
        in_specs=[hbm] * 8,
        out_specs=vmem,
        scratch_shapes=[
            pltpu.SMEM(frame_counts.shape, jnp.int32),
            pltpu.VMEM((C,), F32),
            pltpu.VMEM((C,), F32),
            pltpu.VMEM((half,), F32),
            pltpu.VMEM((half,), F32),
            pltpu.VMEM((reach + 1, R, SL, width), BF16),
            pltpu.VMEM(((reach + 1) * R, SL, width), F32),
            pltpu.VMEM((len(sets), FL * COLS, kpad), F32),
            pltpu.VMEM((R, 3 * kpad, C), BF16),
            pltpu.VMEM((R, FA * COLS, C), F32),
            pltpu.VMEM((R + extra, FA * COLS, C), BF16),
            pltpu.VMEM((R + extra, SL * COLS, C), BF16),
            pltpu.VMEM((3, nin, 3, half, C), BF16),
            pltpu.VMEM((R, 2 * SL, half), F32),
            pltpu.SemaphoreType.DMA((reach + 1, R)),
            pltpu.SemaphoreType.DMA((reach + 1, R)),
            pltpu.SemaphoreType.DMA((R,)),
            pltpu.SemaphoreType.DMA((R,)),
            pltpu.SemaphoreType.DMA((3,)),
            pltpu.SemaphoreType.DMA((R, 3)),
            pltpu.SemaphoreType.DMA((6,)),
        ],
        compiler_params=pltpu.CompilerParams(
            collective_id=0, has_side_effects=True, vmem_limit_bytes=40 * 1024 * 1024
        ),
    )(*[pltpu.with_memory_space_constraint(z, pltpu.HBM) for z in (
        frame_counts,
        latents.reshape(SL, width),
        w_in.reshape(3, 9 * LAT, C),
        gain_in,
        shift_in,
        jnp.swapaxes(w_mid, 3, 4),
        gain_out,
        shift_out,
    )])
    return jnp.swapaxes(raw, 1, 2)[:, None]


def solution(mesh):
    return jax.shard_map(
        shards,
        mesh=mesh,
        in_specs=(
            P(("video", "block"), "band", None),
            P("video"),
            P(),
            P(),
            P(),
            P(None, None, None, None, "chan"),
            P("chan"),
            P("chan"),
        ),
        out_specs=P(("video", "block"), "band", None, "chan"),
        check_vma=False,
    )
```

```python
import functools

import jax
import jax.numpy as jnp
from jax import lax
from jax.experimental import pallas as pl
from jax.experimental.pallas import tpu as pltpu
from jax.sharding import PartitionSpec as P

LAT = 16
C = 384
GROUPS = 32
GW = C // GROUPS
EPSILON = 1e-06
MESH = pl.DeviceIdType.MESH
F32 = jnp.float32
BF16 = jnp.bfloat16


def up(n, m):
    return (n + m - 1) // m * m


def rows_for(r, R):
    return tuple(range(max(0, r - 1), min(R - 1, r + 1) + 1))


def group_matrix(n, width):
    a = lax.broadcasted_iota(jnp.int32, (n, n), 0)
    b = lax.broadcasted_iota(jnp.int32, (n, n), 1)
    for q in range(n // width - 1, 0, -1):
        a = jnp.where(a >= q * width, a - q * width, a)
        b = jnp.where(b >= q * width, b - q * width, b)
    same = ((a * 5462) >> 16) == ((b * 5462) >> 16)
    return jnp.where(same, 1.0, 0.0).astype(BF16)


def group_sums(x, gmat):
    hi = x.astype(BF16)
    rest = x - hi.astype(F32)
    mid = rest.astype(BF16)
    lo = (rest - mid.astype(F32)).astype(BF16)
    n = x.shape[0]
    y = jnp.dot(
        jnp.concatenate([hi, mid, lo], axis=0), gmat, preferred_element_type=F32
    )
    return y[:n] + y[n : 2 * n] + y[2 * n :]


def silu_twice(v):
    return v + v * jnp.tanh(v)


def body(
    nb, R, COLS, SL, reach,
    cnt_hbm, lat_ref, win_ref, gin_hbm, sin_hbm, wmid_ref, gout_hbm, sout_hbm,
    out_ref,
    cnt_ref, gin_ref, sin_ref, gout_ref, sout_ref,
    slots, xf, gf, wpad, c1s, la, lb, wv,
    send_sem, pass_sem, recv_sem, w_sem, win_sem, in_sem,
):
    k = lax.axis_index("block")
    b = lax.axis_index("band")
    half = out_ref.shape[1]
    FL = SL + 4
    FA = SL + 2

    wcopies = []
    for t in range(3):
        c = pltpu.make_async_copy(
            wmid_ref.at[t], wv.at[t], w_sem.at[t]
        )
        wcopies.append(c)
    wincopies = []
    kpad = wpad.shape[1] // 3
    for r in range(R):
        rows = rows_for(r, R)
        first = (rows[0] - r + 1) * 3 * LAT
        size = len(rows) * 3 * LAT
        for t in range(3):
            c = pltpu.make_async_copy(
                win_ref.at[t, pl.ds(first, size)],
                wpad.at[r, pl.ds(t * kpad + rows[0] * 3 * LAT, size)],
                win_sem.at[r, t],
            )
            wincopies.append(c)
    barrier = pltpu.get_barrier_semaphore()
    odd = lax.rem(k, 2) == 1
    for d in range(reach + 1):
        from_there = k >= d if d < 2 else (k >= d) & (lax.rem(k + d, 2) == 1)
        @pl.when(from_there)
        def _():
            for o in range(1 if d == 0 else 0, R):
                pl.semaphore_signal(
                    barrier, inc=1,
                    device_id={"block": k - d, "band": lax.rem(b + R - o, R)},
                    device_id_type=MESH,
                )
    small = [
        pltpu.make_async_copy(src, dst, in_sem.at[i])
        for i, (src, dst) in enumerate(
            [
                (lat_ref, slots.at[0, b]), (cnt_hbm, cnt_ref), (gin_hbm, gin_ref),
                (sin_hbm, sin_ref), (gout_hbm, gout_ref), (sout_hbm, sout_ref),
            ]
        )
    ]
    for c in small + wincopies + wcopies:
        c.start()
    for r in range(R):
        rows = rows_for(r, R)
        lo, hi = rows[0] * 3 * LAT, (rows[-1] + 1) * 3 * LAT
        for t in range(3):
            if lo:
                wpad[r, t * kpad : t * kpad + lo, :] = jnp.zeros((lo, C), BF16)
            if hi < kpad:
                wpad[r, t * kpad + hi : (t + 1) * kpad, :] = jnp.zeros((kpad - hi, C), BF16)
    def copy_to(d, o, passed=False):
        return pltpu.make_async_remote_copy(
            src_ref=slots.at[1 if passed else 0, b],
            dst_ref=slots.at[d, b],
            send_sem=(pass_sem if passed else send_sem).at[d, o],
            recv_sem=recv_sem.at[d, o],
            device_id={"block": k + d - (1 if passed else 0), "band": lax.rem(b + o, R)},
            device_id_type=MESH,
        )

    def copy_from(d, o):
        return pltpu.make_async_remote_copy(
            src_ref=slots.at[0, b],
            dst_ref=slots.at[d, lax.rem(b + R - o, R)],
            send_sem=send_sem.at[d, o],
            recv_sem=recv_sem.at[d, o],
            device_id={"block": k, "band": lax.rem(b + o, R)},
            device_id_type=MESH,
        )

    def sends(d):
        return k + d < nb if d < 2 else (k + d < nb) & odd

    def passes(d):
        return (k + d - 1 < nb) & odd

    a = lax.broadcasted_iota(jnp.int32, (R * 3 * 128, kpad), 0)
    c = lax.broadcasted_iota(jnp.int32, (R * 3 * 128, kpad), 1)
    sel = jnp.where(((a >> 7) * LAT + (a & (LAT - 1))) == c, 1.0, 0.0).astype(BF16)
    gmat = group_matrix(C, C)
    gmat2 = group_matrix(R * half, half)

    small[0].wait()
    peers = R - 1
    for d in range(1, reach + 1):
        peers = peers + jnp.where(sends(d), R, 0)
    pl.semaphore_wait(barrier, peers)
    for d in range(reach, -1, -1):
        @pl.when(sends(d))
        def _():
            for o in range(1 if d == 0 else 0, R):
                copy_to(d, o).start()
    small[1].wait()
    e = [jnp.int32(0)]
    for d in range(1, reach + 1):
        n = cnt_ref[jnp.maximum(k - d, 0)]
        e.append(e[-1] + jnp.where(k >= d, n, 0))
    before = e[-1]
    live = cnt_ref[k]

    def unpack(d):
        for r in range(R):
            xf[d * R + r] = slots[d, r].astype(F32)

    for o in range(1, R):
        copy_from(0, o).wait_recv()
    unpack(0)

    def earlier():
        for d in range(1, reach + 1):
            @pl.when(k >= d)
            def _():
                copy_from(d, 0).wait_recv()
            if d == 1:
                for e_ in range(2, reach + 1):
                    @pl.when(passes(e_))
                    def _():
                        for o in range(R):
                            copy_to(e_, o, True).start()
        for d in range(1, reach + 1):
            @pl.when(k >= d)
            def _():
                for o in range(1, R):
                    copy_from(d, o).wait_recv()
            unpack(d)

    W = COLS * LAT
    lane = lax.broadcasted_iota(jnp.int32, (8, W), 1)
    sub = lax.broadcasted_iota(jnp.int32, (8, W), 0)
    part = (lane >> 4) & 7
    mask = [part == ((sub + 7) & 7), part == sub, part == ((sub + 1) & 7)]
    zero128 = jnp.zeros((8, 128), F32)

    def expanded(j, r):
        if j >= 4:
            row = xf[r, j - 4 : j - 3, :]
        else:
            m = 4 - j
            d = jnp.int32(1)
            base = e[1]
            for q in range(1, reach):
                more = e[q] < m
                d = jnp.where(more, q + 1, d)
                base = jnp.where(more, e[q + 1], base)
            slot = jnp.clip(base - m, 0, SL - 1)
            row = xf[d * R + r, pl.ds(slot, 1), :]
            row = jnp.where(jnp.broadcast_to(before >= m, row.shape), row, 0.0)
        bc = jnp.broadcast_to(row, (8, W))
        prev = jnp.concatenate([zero128, bc[:, : W - 128]], axis=1)
        nxt = jnp.concatenate([bc[:, 128:], zero128], axis=1)
        ys = [
            jnp.where(mask[0], jnp.where(sub == 0, prev, bc), 0.0),
            jnp.where(mask[1], bc, 0.0),
            jnp.where(mask[2], jnp.where(sub == 7, nxt, bc), 0.0),
        ]
        return [
            jnp.concatenate([y[:, q * 128 : q * 128 + 128] for q in range(W // 128)], axis=0)
            for y in ys
        ]

    for p in reversed(range(FL // 2)):
        if p == 1:
            earlier()
        ex = {}
        for r in range(R):
            u, v = expanded(2 * p, r), expanded(2 * p + 1, r)
            ex[r] = [jnp.concatenate([u[x], v[x]], axis=0).astype(BF16) for x in range(3)]
        lhs = jnp.concatenate([ex[r][x] for r in range(R) for x in range(3)], axis=1)
        gf[p * 2 * COLS : (p + 1) * 2 * COLS, :] = jnp.dot(
            lhs, sel, preferred_element_type=F32
        )

    for c in wincopies:
        c.wait()
    MA = FA * COLS
    lhs = jnp.concatenate(
        [gf[t * COLS : t * COLS + MA, :] for t in range(3)], axis=1
    ).astype(BF16)
    rhs = jnp.concatenate([wpad[r] for r in range(R)], axis=1)
    y = jnp.dot(lhs, rhs, preferred_element_type=F32).astype(BF16).astype(F32)
    for r in range(R):
        c1s[r] = y[:, r * C : (r + 1) * C]

    s1, s2 = [], []
    for f in range(FA):
        a1 = a2 = None
        for r in range(R):
            h = c1s[r, f * COLS : (f + 1) * COLS, :]
            p1 = jnp.sum(h, axis=0, keepdims=True)
            p2 = jnp.sum(h * h, axis=0, keepdims=True)
            a1 = p1 if a1 is None else a1 + p1
            a2 = p2 if a2 is None else a2 + p2
        s1.append(a1)
        s2.append(a2)
    fill = jnp.zeros((16 - 2 * FA, C), F32)
    g = group_sums(jnp.concatenate(s1 + s2 + [fill], axis=0), gmat)
    total = float(R * COLS * GW)
    mean = g[:FA] / total
    var = g[FA : 2 * FA] / total - mean * mean
    inv = lax.rsqrt(var + EPSILON)
    for c in small[2:]:
        c.wait()
    scale = inv * (0.5 * gin_ref[...].reshape(1, C))
    shift = 0.5 * sin_ref[...].reshape(1, C) - mean * scale

    for r in range(R):
        act = []
        for f in range(FA):
            u = c1s[r, f * COLS : (f + 1) * COLS, :] * scale[f : f + 1] + shift[f : f + 1]
            a = silu_twice(u)
            if f < 2:
                a = jnp.where(jnp.broadcast_to(before >= 2 - f, a.shape), a, 0.0)
            act.append(a)
        for p in range(FA // 2):
            la[r, p * 2 * COLS : (p + 1) * 2 * COLS, :] = jnp.concatenate(
                act[2 * p : 2 * p + 2], axis=0
            ).astype(BF16)
        for p in range(SL // 2):
            lb[r, p * 2 * COLS : (p + 1) * 2 * COLS, :] = jnp.concatenate(
                act[2 * p + 1 : 2 * p + 3], axis=0
            ).astype(BF16)

    for c in wcopies:
        c.wait()
    M = SL * COLS
    wide = R * half
    lhs = []
    for t in range(3):
        for q in range(R):
            lhs.append(lb[q] if t == 1 else la[q, t * COLS : t * COLS + M, :])
    lhs = jnp.concatenate(lhs, axis=1)

    def taps(t, q, r, x):
        if 0 <= q - r + 1 <= 2:
            return wv[t, q - r + 1, x]
        return jnp.zeros((half, C), BF16)

    rhs = jnp.concatenate(
        [
            jnp.concatenate([taps(t, q, r, x) for t in range(3) for q in range(R)], axis=1)
            for x in range(3)
            for r in range(R)
        ],
        axis=0,
    )
    prod = lax.dot_general(lhs, rhs, (((1,), (1,)), ((), ())), preferred_element_type=F32)
    hs, t1, t2 = [], [], []
    col = lax.broadcasted_iota(jnp.int32, (COLS, wide), 0)
    for f in range(SL):
        p0, p1, p2 = [
            prod[f * COLS : (f + 1) * COLS, x * wide : (x + 1) * wide] for x in range(3)
        ]
        h = p1 + jnp.where(col == 0, 0.0, pltpu.roll(p0, 1, 0))
        h = h + jnp.where(col == COLS - 1, 0.0, pltpu.roll(p2, COLS - 1, 0))
        h = h.astype(BF16).astype(F32)
        hs.append(h)
        t1.append(jnp.sum(h, axis=0, keepdims=True))
        t2.append(jnp.sum(h * h, axis=0, keepdims=True))
    pad = jnp.zeros((16 - 2 * SL, wide), F32)
    g = group_sums(jnp.concatenate(t1 + t2 + [pad], axis=0), gmat2)
    mean = g[:SL] / total
    var = g[SL : 2 * SL] / total - mean * mean
    inv = lax.rsqrt(var + EPSILON)
    gains = jnp.concatenate([0.5 * gout_ref[...].reshape(1, half)] * R, axis=1)
    shifts = jnp.concatenate([0.5 * sout_ref[...].reshape(1, half)] * R, axis=1)
    scale = inv * gains
    shift = shifts - mean * scale
    for r in range(R):
        lo = r * half // 128 * 128
        hi = min(up((r + 1) * half, 128), wide)

        @pl.when(b == r)
        def _():
            for f in range(SL):
                u = hs[f][:, lo:hi] * scale[f : f + 1, lo:hi] + shift[f : f + 1, lo:hi]
                a = silu_twice(u)
                a = jnp.where(jnp.broadcast_to(f < live, a.shape), a, 0.0)
                out_ref[f] = a.T[r * half - lo : (r + 1) * half - lo].astype(BF16)

    for o in range(1, R):
        copy_to(0, o).wait_send()
    for d in range(1, reach + 1):
        @pl.when(sends(d))
        def _():
            for o in range(R):
                copy_to(d, o).wait_send()
    for d in range(2, reach + 1):
        @pl.when(passes(d))
        def _():
            for o in range(R):
                copy_to(d, o, True).wait_send()


def shards(latents, frame_counts, w_in, gain_in, shift_in, w_mid, gain_out, shift_out):
    SL, band_rows, width = latents.shape
    COLS = width // LAT
    half = w_mid.shape[4]
    R = lax.axis_size("band") * band_rows
    nb = lax.axis_size("block")
    reach = min(4, nb - 1)
    FL, FA = SL + 4, SL + 2
    kpad = up(R * 3 * LAT, 128)
    vmem = pl.BlockSpec(memory_space=pltpu.VMEM)
    hbm = pl.BlockSpec(memory_space=pltpu.HBM)
    raw = pl.pallas_call(
        functools.partial(body, nb, R, COLS, SL, reach),
        out_shape=pltpu.VMEM((SL, half, COLS), BF16),
        in_specs=[hbm] * 8,
        out_specs=vmem,
        scratch_shapes=[
            pltpu.SMEM(frame_counts.shape, jnp.int32),
            pltpu.VMEM((C,), F32),
            pltpu.VMEM((C,), F32),
            pltpu.VMEM((half,), F32),
            pltpu.VMEM((half,), F32),
            pltpu.VMEM((reach + 1, R, SL, width), BF16),
            pltpu.VMEM(((reach + 1) * R, SL, width), F32),
            pltpu.VMEM((FL * COLS, kpad), F32),
            pltpu.VMEM((R, 3 * kpad, C), BF16),
            pltpu.VMEM((R, FA * COLS, C), F32),
            pltpu.VMEM((R, FA * COLS, C), BF16),
            pltpu.VMEM((R, SL * COLS, C), BF16),
            pltpu.VMEM((3, 3, 3, half, C), BF16),
            pltpu.SemaphoreType.DMA((reach + 1, R)),
            pltpu.SemaphoreType.DMA((reach + 1, R)),
            pltpu.SemaphoreType.DMA((reach + 1, R)),
            pltpu.SemaphoreType.DMA((3,)),
            pltpu.SemaphoreType.DMA((R, 3)),
            pltpu.SemaphoreType.DMA((6,)),
        ],
        compiler_params=pltpu.CompilerParams(
            collective_id=0, has_side_effects=True, vmem_limit_bytes=40 * 1024 * 1024
        ),
    )(*[pltpu.with_memory_space_constraint(z, pltpu.HBM) for z in (
        frame_counts,
        latents.reshape(SL, width),
        w_in.reshape(3, 9 * LAT, C),
        gain_in,
        shift_in,
        jnp.swapaxes(w_mid, 3, 4),
        gain_out,
        shift_out,
    )])
    return jnp.swapaxes(raw, 1, 2)[:, None]


def solution(mesh):
    return jax.shard_map(
        shards,
        mesh=mesh,
        in_specs=(
            P(("video", "block"), "band", None),
            P("video"),
            P(),
            P(),
            P(),
            P(None, None, None, None, "chan"),
            P("chan"),
            P("chan"),
        ),
        out_specs=P(("video", "block"), "band", None, "chan"),
        check_vma=False,
    )
```

```python
import functools

import jax
import jax.numpy as jnp
from jax import lax
from jax.experimental import pallas as pl
from jax.experimental.pallas import tpu as pltpu
from jax.sharding import PartitionSpec as P

LAT = 16
C = 384
GROUPS = 32
GW = C // GROUPS
EPSILON = 1e-06
MESH = pl.DeviceIdType.MESH
F32 = jnp.float32
BF16 = jnp.bfloat16


def up(n, m):
    return (n + m - 1) // m * m


def rows_for(r, R):
    return tuple(range(max(0, r - 1), min(R - 1, r + 1) + 1))


def group_matrix(n, width):
    a = lax.broadcasted_iota(jnp.int32, (n, n), 0)
    b = lax.broadcasted_iota(jnp.int32, (n, n), 1)
    for q in range(n // width - 1, 0, -1):
        a = jnp.where(a >= q * width, a - q * width, a)
        b = jnp.where(b >= q * width, b - q * width, b)
    same = ((a * 5462) >> 16) == ((b * 5462) >> 16)
    return jnp.where(same, 1.0, 0.0).astype(BF16)


def group_sums(x, gmat):
    hi = x.astype(BF16)
    rest = x - hi.astype(F32)
    mid = rest.astype(BF16)
    lo = (rest - mid.astype(F32)).astype(BF16)
    n = x.shape[0]
    y = jnp.dot(
        jnp.concatenate([hi, mid, lo], axis=0), gmat, preferred_element_type=F32
    )
    return y[:n] + y[n : 2 * n] + y[2 * n :]


def silu_twice(v):
    return v + v * jnp.tanh(v)


def body(
    nb, R, COLS, SL, reach,
    cnt_hbm, lat_ref, win_ref, gin_hbm, sin_hbm, wmid_ref, gout_hbm, sout_hbm,
    out_ref,
    cnt_ref, gin_ref, sin_ref, gout_ref, sout_ref,
    slots, xf, gf, wpad, c1s, la, lb, wv,
    send_sem, pass_sem, recv_sem, w_sem, win_sem, in_sem,
):
    k = lax.axis_index("block")
    b = lax.axis_index("band")
    half = out_ref.shape[1]
    FL = SL + 4
    FA = SL + 2

    wcopies = []
    for t in range(3):
        c = pltpu.make_async_copy(
            wmid_ref.at[t], wv.at[t], w_sem.at[t]
        )
        wcopies.append(c)
    wincopies = []
    kpad = wpad.shape[1] // 3
    for r in range(R):
        rows = rows_for(r, R)
        first = (rows[0] - r + 1) * 3 * LAT
        size = len(rows) * 3 * LAT
        for t in range(3):
            c = pltpu.make_async_copy(
                win_ref.at[t, pl.ds(first, size)],
                wpad.at[r, pl.ds(t * kpad + rows[0] * 3 * LAT, size)],
                win_sem.at[r, t],
            )
            wincopies.append(c)
    barrier = pltpu.get_barrier_semaphore()
    odd = lax.rem(k, 2) == 1
    for d in range(reach + 1):
        from_there = k >= d if d < 2 else (k >= d) & (lax.rem(k + d, 2) == 1)
        @pl.when(from_there)
        def _():
            for o in range(1 if d == 0 else 0, R):
                pl.semaphore_signal(
                    barrier, inc=1,
                    device_id={"block": k - d, "band": lax.rem(b + R - o, R)},
                    device_id_type=MESH,
                )
    small = [
        pltpu.make_async_copy(src, dst, in_sem.at[i])
        for i, (src, dst) in enumerate(
            [
                (lat_ref, slots.at[0, b]), (cnt_hbm, cnt_ref), (gin_hbm, gin_ref),
                (sin_hbm, sin_ref), (gout_hbm, gout_ref), (sout_hbm, sout_ref),
            ]
        )
    ]
    for c in small + wincopies + wcopies:
        c.start()
    for r in range(R):
        rows = rows_for(r, R)
        lo, hi = rows[0] * 3 * LAT, (rows[-1] + 1) * 3 * LAT
        for t in range(3):
            if lo:
                wpad[r, t * kpad : t * kpad + lo, :] = jnp.zeros((lo, C), BF16)
            if hi < kpad:
                wpad[r, t * kpad + hi : (t + 1) * kpad, :] = jnp.zeros((kpad - hi, C), BF16)
    def copy_to(d, o, passed=False):
        return pltpu.make_async_remote_copy(
            src_ref=slots.at[1 if passed else 0, b],
            dst_ref=slots.at[d, b],
            send_sem=(pass_sem if passed else send_sem).at[d, o],
            recv_sem=recv_sem.at[d, o],
            device_id={"block": k + d - (1 if passed else 0), "band": lax.rem(b + o, R)},
            device_id_type=MESH,
        )

    def copy_from(d, o):
        return pltpu.make_async_remote_copy(
            src_ref=slots.at[0, b],
            dst_ref=slots.at[d, lax.rem(b + R - o, R)],
            send_sem=send_sem.at[d, o],
            recv_sem=recv_sem.at[d, o],
            device_id={"block": k, "band": lax.rem(b + o, R)},
            device_id_type=MESH,
        )

    def sends(d):
        return k + d < nb if d < 2 else (k + d < nb) & odd

    def passes(d):
        return (k + d - 1 < nb) & odd

    a = lax.broadcasted_iota(jnp.int32, (R * 3 * 128, kpad), 0)
    c = lax.broadcasted_iota(jnp.int32, (R * 3 * 128, kpad), 1)
    sel = jnp.where(((a >> 7) * LAT + (a & (LAT - 1))) == c, 1.0, 0.0).astype(BF16)
    gmat = group_matrix(C, C)
    gmat2 = group_matrix(R * half, half)

    small[0].wait()
    peers = R - 1
    for d in range(1, reach + 1):
        peers = peers + jnp.where(sends(d), R, 0)
    pl.semaphore_wait(barrier, peers)
    for d in range(reach, -1, -1):
        @pl.when(sends(d))
        def _():
            for o in range(1 if d == 0 else 0, R):
                copy_to(d, o).start()

    @pl.when(odd)
    def _():
        copy_from(1, 0).wait_recv()
        for d in range(reach, 1, -1):
            @pl.when(passes(d))
            def _():
                for o in range(R):
                    copy_to(d, o, True).start()

    small[1].wait()
    e = [jnp.int32(0)]
    for d in range(1, reach + 1):
        n = cnt_ref[jnp.maximum(k - d, 0)]
        e.append(e[-1] + jnp.where(k >= d, n, 0))
    before = e[-1]
    live = cnt_ref[k]

    def unpack(d):
        for r in range(R):
            xf[d * R + r] = slots[d, r].astype(F32)

    for o in range(1, R):
        copy_from(0, o).wait_recv()
    unpack(0)

    def earlier():
        for d in range(1, reach + 1):
            @pl.when((k >= d) & ~odd if d == 1 else k >= d)
            def _():
                copy_from(d, 0).wait_recv()
        for d in range(1, reach + 1):
            @pl.when(k >= d)
            def _():
                for o in range(1, R):
                    copy_from(d, o).wait_recv()
            unpack(d)

    W = COLS * LAT
    lane = lax.broadcasted_iota(jnp.int32, (8, W), 1)
    sub = lax.broadcasted_iota(jnp.int32, (8, W), 0)
    part = (lane >> 4) & 7
    mask = [part == ((sub + 7) & 7), part == sub, part == ((sub + 1) & 7)]
    zero128 = jnp.zeros((8, 128), F32)

    def expanded(j, r):
        if j >= 4:
            row = xf[r, j - 4 : j - 3, :]
        else:
            m = 4 - j
            d = jnp.int32(1)
            base = e[1]
            for q in range(1, reach):
                more = e[q] < m
                d = jnp.where(more, q + 1, d)
                base = jnp.where(more, e[q + 1], base)
            slot = jnp.clip(base - m, 0, SL - 1)
            row = xf[d * R + r, pl.ds(slot, 1), :]
            row = jnp.where(jnp.broadcast_to(before >= m, row.shape), row, 0.0)
        bc = jnp.broadcast_to(row, (8, W))
        prev = jnp.concatenate([zero128, bc[:, : W - 128]], axis=1)
        nxt = jnp.concatenate([bc[:, 128:], zero128], axis=1)
        ys = [
            jnp.where(mask[0], jnp.where(sub == 0, prev, bc), 0.0),
            jnp.where(mask[1], bc, 0.0),
            jnp.where(mask[2], jnp.where(sub == 7, nxt, bc), 0.0),
        ]
        return [
            jnp.concatenate([y[:, q * 128 : q * 128 + 128] for q in range(W // 128)], axis=0)
            for y in ys
        ]

    for p in reversed(range(FL // 2)):
        if p == 1:
            earlier()
        ex = {}
        for r in range(R):
            u, v = expanded(2 * p, r), expanded(2 * p + 1, r)
            ex[r] = [jnp.concatenate([u[x], v[x]], axis=0).astype(BF16) for x in range(3)]
        lhs = jnp.concatenate([ex[r][x] for r in range(R) for x in range(3)], axis=1)
        gf[p * 2 * COLS : (p + 1) * 2 * COLS, :] = jnp.dot(
            lhs, sel, preferred_element_type=F32
        )

    for c in wincopies:
        c.wait()
    MA = FA * COLS
    lhs = jnp.concatenate(
        [gf[t * COLS : t * COLS + MA, :] for t in range(3)], axis=1
    ).astype(BF16)
    rhs = jnp.concatenate([wpad[r] for r in range(R)], axis=1)
    y = jnp.dot(lhs, rhs, preferred_element_type=F32).astype(BF16).astype(F32)
    for r in range(R):
        c1s[r] = y[:, r * C : (r + 1) * C]

    s1, s2 = [], []
    for f in range(FA):
        a1 = a2 = None
        for r in range(R):
            h = c1s[r, f * COLS : (f + 1) * COLS, :]
            p1 = jnp.sum(h, axis=0, keepdims=True)
            p2 = jnp.sum(h * h, axis=0, keepdims=True)
            a1 = p1 if a1 is None else a1 + p1
            a2 = p2 if a2 is None else a2 + p2
        s1.append(a1)
        s2.append(a2)
    fill = jnp.zeros((16 - 2 * FA, C), F32)
    g = group_sums(jnp.concatenate(s1 + s2 + [fill], axis=0), gmat)
    total = float(R * COLS * GW)
    mean = g[:FA] / total
    var = g[FA : 2 * FA] / total - mean * mean
    inv = lax.rsqrt(var + EPSILON)
    for c in small[2:]:
        c.wait()
    scale = inv * (0.5 * gin_ref[...].reshape(1, C))
    shift = 0.5 * sin_ref[...].reshape(1, C) - mean * scale

    for r in range(R):
        act = []
        for f in range(FA):
            u = c1s[r, f * COLS : (f + 1) * COLS, :] * scale[f : f + 1] + shift[f : f + 1]
            a = silu_twice(u)
            if f < 2:
                a = jnp.where(jnp.broadcast_to(before >= 2 - f, a.shape), a, 0.0)
            act.append(a)
        for p in range(FA // 2):
            la[r, p * 2 * COLS : (p + 1) * 2 * COLS, :] = jnp.concatenate(
                act[2 * p : 2 * p + 2], axis=0
            ).astype(BF16)
        for p in range(SL // 2):
            lb[r, p * 2 * COLS : (p + 1) * 2 * COLS, :] = jnp.concatenate(
                act[2 * p + 1 : 2 * p + 3], axis=0
            ).astype(BF16)

    for c in wcopies:
        c.wait()
    M = SL * COLS
    wide = R * half
    lhs = []
    for t in range(3):
        for q in range(R):
            lhs.append(lb[q] if t == 1 else la[q, t * COLS : t * COLS + M, :])
    lhs = jnp.concatenate(lhs, axis=1)

    def taps(t, q, r, x):
        if 0 <= q - r + 1 <= 2:
            return wv[t, q - r + 1, x]
        return jnp.zeros((half, C), BF16)

    rhs = jnp.concatenate(
        [
            jnp.concatenate([taps(t, q, r, x) for t in range(3) for q in range(R)], axis=1)
            for x in range(3)
            for r in range(R)
        ],
        axis=0,
    )
    prod = lax.dot_general(lhs, rhs, (((1,), (1,)), ((), ())), preferred_element_type=F32)
    hs, t1, t2 = [], [], []
    col = lax.broadcasted_iota(jnp.int32, (COLS, wide), 0)
    for f in range(SL):
        p0, p1, p2 = [
            prod[f * COLS : (f + 1) * COLS, x * wide : (x + 1) * wide] for x in range(3)
        ]
        h = p1 + jnp.where(col == 0, 0.0, pltpu.roll(p0, 1, 0))
        h = h + jnp.where(col == COLS - 1, 0.0, pltpu.roll(p2, COLS - 1, 0))
        h = h.astype(BF16).astype(F32)
        hs.append(h)
        t1.append(jnp.sum(h, axis=0, keepdims=True))
        t2.append(jnp.sum(h * h, axis=0, keepdims=True))
    pad = jnp.zeros((16 - 2 * SL, wide), F32)
    g = group_sums(jnp.concatenate(t1 + t2 + [pad], axis=0), gmat2)
    mean = g[:SL] / total
    var = g[SL : 2 * SL] / total - mean * mean
    inv = lax.rsqrt(var + EPSILON)
    gains = jnp.concatenate([0.5 * gout_ref[...].reshape(1, half)] * R, axis=1)
    shifts = jnp.concatenate([0.5 * sout_ref[...].reshape(1, half)] * R, axis=1)
    scale = inv * gains
    shift = shifts - mean * scale
    for r in range(R):
        lo = r * half // 128 * 128
        hi = min(up((r + 1) * half, 128), wide)

        @pl.when(b == r)
        def _():
            for f in range(SL):
                u = hs[f][:, lo:hi] * scale[f : f + 1, lo:hi] + shift[f : f + 1, lo:hi]
                a = silu_twice(u)
                a = jnp.where(jnp.broadcast_to(f < live, a.shape), a, 0.0)
                out_ref[f] = a.T[r * half - lo : (r + 1) * half - lo].astype(BF16)

    for o in range(1, R):
        copy_to(0, o).wait_send()
    for d in range(1, reach + 1):
        @pl.when(sends(d))
        def _():
            for o in range(R):
                copy_to(d, o).wait_send()
    for d in range(2, reach + 1):
        @pl.when(passes(d))
        def _():
            for o in range(R):
                copy_to(d, o, True).wait_send()


def shards(latents, frame_counts, w_in, gain_in, shift_in, w_mid, gain_out, shift_out):
    SL, band_rows, width = latents.shape
    COLS = width // LAT
    half = w_mid.shape[4]
    R = lax.axis_size("band") * band_rows
    nb = lax.axis_size("block")
    reach = min(4, nb - 1)
    FL, FA = SL + 4, SL + 2
    kpad = up(R * 3 * LAT, 128)
    vmem = pl.BlockSpec(memory_space=pltpu.VMEM)
    hbm = pl.BlockSpec(memory_space=pltpu.HBM)
    raw = pl.pallas_call(
        functools.partial(body, nb, R, COLS, SL, reach),
        out_shape=pltpu.VMEM((SL, half, COLS), BF16),
        in_specs=[hbm] * 8,
        out_specs=vmem,
        scratch_shapes=[
            pltpu.SMEM(frame_counts.shape, jnp.int32),
            pltpu.VMEM((C,), F32),
            pltpu.VMEM((C,), F32),
            pltpu.VMEM((half,), F32),
            pltpu.VMEM((half,), F32),
            pltpu.VMEM((reach + 1, R, SL, width), BF16),
            pltpu.VMEM(((reach + 1) * R, SL, width), F32),
            pltpu.VMEM((FL * COLS, kpad), F32),
            pltpu.VMEM((R, 3 * kpad, C), BF16),
            pltpu.VMEM((R, FA * COLS, C), F32),
            pltpu.VMEM((R, FA * COLS, C), BF16),
            pltpu.VMEM((R, SL * COLS, C), BF16),
            pltpu.VMEM((3, 3, 3, half, C), BF16),
            pltpu.SemaphoreType.DMA((reach + 1, R)),
            pltpu.SemaphoreType.DMA((reach + 1, R)),
            pltpu.SemaphoreType.DMA((reach + 1, R)),
            pltpu.SemaphoreType.DMA((3,)),
            pltpu.SemaphoreType.DMA((R, 3)),
            pltpu.SemaphoreType.DMA((6,)),
        ],
        compiler_params=pltpu.CompilerParams(
            collective_id=0, has_side_effects=True, vmem_limit_bytes=40 * 1024 * 1024
        ),
    )(*[pltpu.with_memory_space_constraint(z, pltpu.HBM) for z in (
        frame_counts,
        latents.reshape(SL, width),
        w_in.reshape(3, 9 * LAT, C),
        gain_in,
        shift_in,
        jnp.swapaxes(w_mid, 3, 4),
        gain_out,
        shift_out,
    )])
    return jnp.swapaxes(raw, 1, 2)[:, None]


def solution(mesh):
    return jax.shard_map(
        shards,
        mesh=mesh,
        in_specs=(
            P(("video", "block"), "band", None),
            P("video"),
            P(),
            P(),
            P(),
            P(None, None, None, None, "chan"),
            P("chan"),
            P("chan"),
        ),
        out_specs=P(("video", "block"), "band", None, "chan"),
        check_vma=False,
    )
```

```python
import functools

import jax
import jax.numpy as jnp
from jax import lax
from jax.experimental import pallas as pl
from jax.experimental.pallas import tpu as pltpu
from jax.sharding import PartitionSpec as P

LAT = 16
C = 384
GROUPS = 32
GW = C // GROUPS
EPSILON = 1e-06
MESH = pl.DeviceIdType.MESH
F32 = jnp.float32
BF16 = jnp.bfloat16


def up(n, m):
    return (n + m - 1) // m * m


def rows_for(r, R):
    return tuple(range(max(0, r - 1), min(R - 1, r + 1) + 1))


def group_matrix(n, width):
    a = lax.broadcasted_iota(jnp.int32, (n, n), 0)
    b = lax.broadcasted_iota(jnp.int32, (n, n), 1)
    for q in range(n // width - 1, 0, -1):
        a = jnp.where(a >= q * width, a - q * width, a)
        b = jnp.where(b >= q * width, b - q * width, b)
    same = ((a * 5462) >> 16) == ((b * 5462) >> 16)
    return jnp.where(same, 1.0, 0.0).astype(BF16)


def group_sums(x, gmat):
    hi = x.astype(BF16)
    rest = x - hi.astype(F32)
    mid = rest.astype(BF16)
    lo = (rest - mid.astype(F32)).astype(BF16)
    n = x.shape[0]
    y = jnp.dot(
        jnp.concatenate([hi, mid, lo], axis=0), gmat, preferred_element_type=F32
    )
    return y[:n] + y[n : 2 * n] + y[2 * n :]


def silu_twice(v):
    return v + v * jnp.tanh(v)


def body(
    nb, R, COLS, SL, reach,
    cnt_hbm, lat_ref, win_ref, gin_hbm, sin_hbm, wmid_ref, gout_hbm, sout_hbm,
    out_ref,
    cnt_ref, gin_ref, sin_ref, gout_ref, sout_ref,
    slots, xf, gf, wpad, c1s, la, lb, wv,
    send_sem, pass_sem, recv_sem, w_sem, win_sem, in_sem,
):
    k = lax.axis_index("block")
    b = lax.axis_index("band")
    cores = lax.axis_size("chan")
    speaks = lax.axis_index("chan") == cores - 1
    half = out_ref.shape[1]
    FL = SL + 4
    FA = SL + 2

    wcopies = []
    for t in range(3):
        c = pltpu.make_async_copy(
            wmid_ref.at[t], wv.at[t], w_sem.at[t]
        )
        wcopies.append(c)
    wincopies = []
    kpad = wpad.shape[1] // 3
    for r in range(R):
        rows = rows_for(r, R)
        first = (rows[0] - r + 1) * 3 * LAT
        size = len(rows) * 3 * LAT
        for t in range(3):
            c = pltpu.make_async_copy(
                win_ref.at[t, pl.ds(first, size)],
                wpad.at[r, pl.ds(t * kpad + rows[0] * 3 * LAT, size)],
                win_sem.at[r, t],
            )
            wincopies.append(c)
    barrier = pltpu.get_barrier_semaphore()
    odd = lax.rem(k, 2) == 1
    for d in range(reach + 1):
        from_there = k >= d if d < 2 else (k >= d) & (lax.rem(k + d, 2) == 1)
        @pl.when(from_there)
        def _():
            for o in range(1 if d == 0 else 0, R):
                pl.semaphore_signal(
                    barrier, inc=1,
                    device_id={"block": k - d, "band": lax.rem(b + R - o, R), "chan": cores - 1},
                    device_id_type=MESH,
                )
    small = [
        pltpu.make_async_copy(src, dst, in_sem.at[i])
        for i, (src, dst) in enumerate(
            [
                (lat_ref, slots.at[0, b]), (cnt_hbm, cnt_ref), (gin_hbm, gin_ref),
                (sin_hbm, sin_ref), (gout_hbm, gout_ref), (sout_hbm, sout_ref),
            ]
        )
    ]
    for c in small + wincopies + wcopies:
        c.start()
    for r in range(R):
        rows = rows_for(r, R)
        lo, hi = rows[0] * 3 * LAT, (rows[-1] + 1) * 3 * LAT
        for t in range(3):
            if lo:
                wpad[r, t * kpad : t * kpad + lo, :] = jnp.zeros((lo, C), BF16)
            if hi < kpad:
                wpad[r, t * kpad + hi : (t + 1) * kpad, :] = jnp.zeros((kpad - hi, C), BF16)
    def copy_to(d, o, c, passed=False):
        return pltpu.make_async_remote_copy(
            src_ref=slots.at[1 if passed else 0, b],
            dst_ref=slots.at[d, b],
            send_sem=(pass_sem if passed else send_sem).at[d, o, c],
            recv_sem=recv_sem.at[d, o],
            device_id={
                "block": k + d - (1 if passed else 0),
                "band": lax.rem(b + o, R),
                "chan": c,
            },
            device_id_type=MESH,
        )

    def copy_from(d, o):
        return pltpu.make_async_remote_copy(
            src_ref=slots.at[0, b],
            dst_ref=slots.at[d, lax.rem(b + R - o, R)],
            send_sem=send_sem.at[d, o, 0],
            recv_sem=recv_sem.at[d, o],
            device_id={"block": k, "band": lax.rem(b + o, R)},
            device_id_type=MESH,
        )

    def sends(d):
        return speaks & (k + d < nb if d < 2 else (k + d < nb) & odd)

    def passes(d):
        return speaks & (k + d - 1 < nb) & odd

    a = lax.broadcasted_iota(jnp.int32, (R * 3 * 128, kpad), 0)
    c = lax.broadcasted_iota(jnp.int32, (R * 3 * 128, kpad), 1)
    sel = jnp.where(((a >> 7) * LAT + (a & (LAT - 1))) == c, 1.0, 0.0).astype(BF16)
    gmat = group_matrix(C, C)
    gmat2 = group_matrix(R * half, half)

    small[0].wait()
    peers = jnp.int32(R - 1)
    for d in range(1, reach + 1):
        peers = peers + jnp.where(sends(d), R, 0)
    @pl.when(speaks)
    def _():
        pl.semaphore_wait(barrier, peers * cores)

    for d in range(reach, -1, -1):
        @pl.when(sends(d))
        def _():
            for o in range(1 if d == 0 else 0, R):
                for c in range(cores):
                    copy_to(d, o, c).start()

    @pl.when(odd & speaks)
    def _():
        copy_from(1, 0).wait_recv()
        for d in range(reach, 1, -1):
            @pl.when(passes(d))
            def _():
                for o in range(R):
                    for c in range(cores):
                        copy_to(d, o, c, True).start()

    small[1].wait()
    e = [jnp.int32(0)]
    for d in range(1, reach + 1):
        n = cnt_ref[jnp.maximum(k - d, 0)]
        e.append(e[-1] + jnp.where(k >= d, n, 0))
    before = e[-1]
    live = cnt_ref[k]

    def unpack(d):
        for r in range(R):
            xf[d * R + r] = slots[d, r].astype(F32)

    for o in range(1, R):
        copy_from(0, o).wait_recv()
    unpack(0)

    def earlier():
        for d in range(1, reach + 1):
            @pl.when((k >= d) & ~(odd & speaks) if d == 1 else k >= d)
            def _():
                copy_from(d, 0).wait_recv()
        for d in range(1, reach + 1):
            @pl.when(k >= d)
            def _():
                for o in range(1, R):
                    copy_from(d, o).wait_recv()
            unpack(d)

    W = COLS * LAT
    lane = lax.broadcasted_iota(jnp.int32, (8, W), 1)
    sub = lax.broadcasted_iota(jnp.int32, (8, W), 0)
    part = (lane >> 4) & 7
    mask = [part == ((sub + 7) & 7), part == sub, part == ((sub + 1) & 7)]
    zero128 = jnp.zeros((8, 128), F32)

    def expanded(j, r):
        if j >= 4:
            row = xf[r, j - 4 : j - 3, :]
        else:
            m = 4 - j
            d = jnp.int32(1)
            base = e[1]
            for q in range(1, reach):
                more = e[q] < m
                d = jnp.where(more, q + 1, d)
                base = jnp.where(more, e[q + 1], base)
            slot = jnp.clip(base - m, 0, SL - 1)
            row = xf[d * R + r, pl.ds(slot, 1), :]
            row = jnp.where(jnp.broadcast_to(before >= m, row.shape), row, 0.0)
        bc = jnp.broadcast_to(row, (8, W))
        prev = jnp.concatenate([zero128, bc[:, : W - 128]], axis=1)
        nxt = jnp.concatenate([bc[:, 128:], zero128], axis=1)
        ys = [
            jnp.where(mask[0], jnp.where(sub == 0, prev, bc), 0.0),
            jnp.where(mask[1], bc, 0.0),
            jnp.where(mask[2], jnp.where(sub == 7, nxt, bc), 0.0),
        ]
        return [
            jnp.concatenate([y[:, q * 128 : q * 128 + 128] for q in range(W // 128)], axis=0)
            for y in ys
        ]

    for p in reversed(range(FL // 2)):
        if p == 1:
            earlier()
        ex = {}
        for r in range(R):
            u, v = expanded(2 * p, r), expanded(2 * p + 1, r)
            ex[r] = [jnp.concatenate([u[x], v[x]], axis=0).astype(BF16) for x in range(3)]
        lhs = jnp.concatenate([ex[r][x] for r in range(R) for x in range(3)], axis=1)
        gf[p * 2 * COLS : (p + 1) * 2 * COLS, :] = jnp.dot(
            lhs, sel, preferred_element_type=F32
        )

    for c in wincopies:
        c.wait()
    MA = FA * COLS
    lhs = jnp.concatenate(
        [gf[t * COLS : t * COLS + MA, :] for t in range(3)], axis=1
    ).astype(BF16)
    rhs = jnp.concatenate([wpad[r] for r in range(R)], axis=1)
    y = jnp.dot(lhs, rhs, preferred_element_type=F32).astype(BF16).astype(F32)
    for r in range(R):
        c1s[r] = y[:, r * C : (r + 1) * C]

    s1, s2 = [], []
    for f in range(FA):
        a1 = a2 = None
        for r in range(R):
            h = c1s[r, f * COLS : (f + 1) * COLS, :]
            p1 = jnp.sum(h, axis=0, keepdims=True)
            p2 = jnp.sum(h * h, axis=0, keepdims=True)
            a1 = p1 if a1 is None else a1 + p1
            a2 = p2 if a2 is None else a2 + p2
        s1.append(a1)
        s2.append(a2)
    fill = jnp.zeros((16 - 2 * FA, C), F32)
    g = group_sums(jnp.concatenate(s1 + s2 + [fill], axis=0), gmat)
    total = float(R * COLS * GW)
    mean = g[:FA] / total
    var = g[FA : 2 * FA] / total - mean * mean
    inv = lax.rsqrt(var + EPSILON)
    for c in small[2:]:
        c.wait()
    scale = inv * (0.5 * gin_ref[...].reshape(1, C))
    shift = 0.5 * sin_ref[...].reshape(1, C) - mean * scale

    for r in range(R):
        act = []
        for f in range(FA):
            u = c1s[r, f * COLS : (f + 1) * COLS, :] * scale[f : f + 1] + shift[f : f + 1]
            a = silu_twice(u)
            if f < 2:
                a = jnp.where(jnp.broadcast_to(before >= 2 - f, a.shape), a, 0.0)
            act.append(a)
        for p in range(FA // 2):
            la[r, p * 2 * COLS : (p + 1) * 2 * COLS, :] = jnp.concatenate(
                act[2 * p : 2 * p + 2], axis=0
            ).astype(BF16)
        for p in range(SL // 2):
            lb[r, p * 2 * COLS : (p + 1) * 2 * COLS, :] = jnp.concatenate(
                act[2 * p + 1 : 2 * p + 3], axis=0
            ).astype(BF16)

    for c in wcopies:
        c.wait()
    M = SL * COLS
    wide = R * half
    lhs = []
    for t in range(3):
        for q in range(R):
            lhs.append(lb[q] if t == 1 else la[q, t * COLS : t * COLS + M, :])
    lhs = jnp.concatenate(lhs, axis=1)

    def taps(t, q, r, x):
        if 0 <= q - r + 1 <= 2:
            return wv[t, q - r + 1, x]
        return jnp.zeros((half, C), BF16)

    rhs = jnp.concatenate(
        [
            jnp.concatenate([taps(t, q, r, x) for t in range(3) for q in range(R)], axis=1)
            for x in range(3)
            for r in range(R)
        ],
        axis=0,
    )
    prod = lax.dot_general(lhs, rhs, (((1,), (1,)), ((), ())), preferred_element_type=F32)
    hs, t1, t2 = [], [], []
    col = lax.broadcasted_iota(jnp.int32, (COLS, wide), 0)
    for f in range(SL):
        p0, p1, p2 = [
            prod[f * COLS : (f + 1) * COLS, x * wide : (x + 1) * wide] for x in range(3)
        ]
        h = p1 + jnp.where(col == 0, 0.0, pltpu.roll(p0, 1, 0))
        h = h + jnp.where(col == COLS - 1, 0.0, pltpu.roll(p2, COLS - 1, 0))
        h = h.astype(BF16).astype(F32)
        hs.append(h)
        t1.append(jnp.sum(h, axis=0, keepdims=True))
        t2.append(jnp.sum(h * h, axis=0, keepdims=True))
    pad = jnp.zeros((16 - 2 * SL, wide), F32)
    g = group_sums(jnp.concatenate(t1 + t2 + [pad], axis=0), gmat2)
    mean = g[:SL] / total
    var = g[SL : 2 * SL] / total - mean * mean
    inv = lax.rsqrt(var + EPSILON)
    gains = jnp.concatenate([0.5 * gout_ref[...].reshape(1, half)] * R, axis=1)
    shifts = jnp.concatenate([0.5 * sout_ref[...].reshape(1, half)] * R, axis=1)
    scale = inv * gains
    shift = shifts - mean * scale
    for r in range(R):
        lo = r * half // 128 * 128
        hi = min(up((r + 1) * half, 128), wide)

        @pl.when(b == r)
        def _():
            for f in range(SL):
                u = hs[f][:, lo:hi] * scale[f : f + 1, lo:hi] + shift[f : f + 1, lo:hi]
                a = silu_twice(u)
                a = jnp.where(jnp.broadcast_to(f < live, a.shape), a, 0.0)
                out_ref[f] = a.T[r * half - lo : (r + 1) * half - lo].astype(BF16)

    for d in range(reach + 1):
        @pl.when(sends(d))
        def _():
            for o in range(1 if d == 0 else 0, R):
                for c in range(cores):
                    copy_to(d, o, c).wait_send()
    for d in range(2, reach + 1):
        @pl.when(passes(d))
        def _():
            for o in range(R):
                for c in range(cores):
                    copy_to(d, o, c, True).wait_send()


def shards(latents, frame_counts, w_in, gain_in, shift_in, w_mid, gain_out, shift_out):
    SL, band_rows, width = latents.shape
    COLS = width // LAT
    half = w_mid.shape[4]
    R = lax.axis_size("band") * band_rows
    nb = lax.axis_size("block")
    cores = lax.axis_size("chan")
    reach = min(4, nb - 1)
    FL, FA = SL + 4, SL + 2
    kpad = up(R * 3 * LAT, 128)
    vmem = pl.BlockSpec(memory_space=pltpu.VMEM)
    hbm = pl.BlockSpec(memory_space=pltpu.HBM)
    raw = pl.pallas_call(
        functools.partial(body, nb, R, COLS, SL, reach),
        out_shape=pltpu.VMEM((SL, half, COLS), BF16),
        in_specs=[hbm] * 8,
        out_specs=vmem,
        scratch_shapes=[
            pltpu.SMEM(frame_counts.shape, jnp.int32),
            pltpu.VMEM((C,), F32),
            pltpu.VMEM((C,), F32),
            pltpu.VMEM((half,), F32),
            pltpu.VMEM((half,), F32),
            pltpu.VMEM((reach + 1, R, SL, width), BF16),
            pltpu.VMEM(((reach + 1) * R, SL, width), F32),
            pltpu.VMEM((FL * COLS, kpad), F32),
            pltpu.VMEM((R, 3 * kpad, C), BF16),
            pltpu.VMEM((R, FA * COLS, C), F32),
            pltpu.VMEM((R, FA * COLS, C), BF16),
            pltpu.VMEM((R, SL * COLS, C), BF16),
            pltpu.VMEM((3, 3, 3, half, C), BF16),
            pltpu.SemaphoreType.DMA((reach + 1, R, cores)),
            pltpu.SemaphoreType.DMA((reach + 1, R, cores)),
            pltpu.SemaphoreType.DMA((reach + 1, R)),
            pltpu.SemaphoreType.DMA((3,)),
            pltpu.SemaphoreType.DMA((R, 3)),
            pltpu.SemaphoreType.DMA((6,)),
        ],
        compiler_params=pltpu.CompilerParams(
            collective_id=0, has_side_effects=True, vmem_limit_bytes=40 * 1024 * 1024
        ),
    )(*[pltpu.with_memory_space_constraint(z, pltpu.HBM) for z in (
        frame_counts,
        latents.reshape(SL, width),
        w_in.reshape(3, 9 * LAT, C),
        gain_in,
        shift_in,
        jnp.swapaxes(w_mid, 3, 4),
        gain_out,
        shift_out,
    )])
    return jnp.swapaxes(raw, 1, 2)[:, None]


def solution(mesh):
    return jax.shard_map(
        shards,
        mesh=mesh,
        in_specs=(
            P(("video", "block"), "band", None),
            P("video"),
            P(),
            P(),
            P(),
            P(None, None, None, None, "chan"),
            P("chan"),
            P("chan"),
        ),
        out_specs=P(("video", "block"), "band", None, "chan"),
        check_vma=False,
    )
```

```python
import functools

import jax
import jax.numpy as jnp
from jax import lax
from jax.experimental import pallas as pl
from jax.experimental.pallas import tpu as pltpu
from jax.sharding import PartitionSpec as P

LAT = 16
C = 384
GROUPS = 32
GW = C // GROUPS
EPSILON = 1e-06
MESH = pl.DeviceIdType.MESH
F32 = jnp.float32
BF16 = jnp.bfloat16


def up(n, m):
    return (n + m - 1) // m * m


def rows_for(r, R):
    return tuple(range(max(0, r - 1), min(R - 1, r + 1) + 1))


def group_matrix(n, width):
    a = lax.broadcasted_iota(jnp.int32, (n, n), 0)
    b = lax.broadcasted_iota(jnp.int32, (n, n), 1)
    for q in range(n // width - 1, 0, -1):
        a = jnp.where(a >= q * width, a - q * width, a)
        b = jnp.where(b >= q * width, b - q * width, b)
    same = ((a * 5462) >> 16) == ((b * 5462) >> 16)
    return jnp.where(same, 1.0, 0.0).astype(BF16)


def group_sums(x, gmat):
    hi = x.astype(BF16)
    rest = x - hi.astype(F32)
    mid = rest.astype(BF16)
    lo = (rest - mid.astype(F32)).astype(BF16)
    n = x.shape[0]
    y = jnp.dot(
        jnp.concatenate([hi, mid, lo], axis=0), gmat, preferred_element_type=F32
    )
    return y[:n] + y[n : 2 * n] + y[2 * n :]


def silu_twice(v):
    return v + v * jnp.tanh(v)


def body(
    nb, R, COLS, SL, reach,
    cnt_hbm, lat_ref, win_ref, gin_hbm, sin_hbm, wmid_ref, gout_hbm, sout_hbm,
    out_ref,
    cnt_ref, gin_ref, sin_ref, gout_ref, sout_ref,
    slots, xf, gf, wpad, c1s, la, lb, wv,
    send_sem, pass_sem, recv_sem, w_sem, win_sem, in_sem,
):
    k = lax.axis_index("block")
    b = lax.axis_index("band")
    cores = lax.axis_size("chan")
    core = lax.axis_index("chan")
    passer = (lax.rem(k, 2) == 1) & (core == cores - 1)
    half = out_ref.shape[1]
    FL = SL + 4
    FA = SL + 2

    wcopies = []
    for t in range(3):
        c = pltpu.make_async_copy(
            wmid_ref.at[t], wv.at[t], w_sem.at[t]
        )
        wcopies.append(c)
    wincopies = []
    kpad = wpad.shape[1] // 3
    for r in range(R):
        rows = rows_for(r, R)
        first = (rows[0] - r + 1) * 3 * LAT
        size = len(rows) * 3 * LAT
        for t in range(3):
            c = pltpu.make_async_copy(
                win_ref.at[t, pl.ds(first, size)],
                wpad.at[r, pl.ds(t * kpad + rows[0] * 3 * LAT, size)],
                win_sem.at[r, t],
            )
            wincopies.append(c)
    barrier = pltpu.get_barrier_semaphore()
    odd = lax.rem(k, 2) == 1
    for d in range(reach + 1):
        from_there = k >= d if d < 2 else (k >= d) & (lax.rem(k + d, 2) == 1)
        @pl.when(from_there)
        def _():
            for o in range(1 if d == 0 else 0, R):
                pl.semaphore_signal(
                    barrier, inc=1,
                    device_id={"block": k - d, "band": lax.rem(b + R - o, R)},
                    device_id_type=MESH,
                )
    for d in range(1, reach):
        @pl.when((k >= d) & (lax.rem(k + d, 2) == 1) & (core < cores - 1))
        def _():
            for o in range(R):
                pl.semaphore_signal(
                    barrier, inc=1,
                    device_id={"block": k - d, "band": lax.rem(b + R - o, R), "chan": cores - 1},
                    device_id_type=MESH,
                )
    small = [
        pltpu.make_async_copy(src, dst, in_sem.at[i])
        for i, (src, dst) in enumerate(
            [
                (lat_ref, slots.at[0, b]), (cnt_hbm, cnt_ref), (gin_hbm, gin_ref),
                (sin_hbm, sin_ref), (gout_hbm, gout_ref), (sout_hbm, sout_ref),
            ]
        )
    ]
    for c in small + wincopies + wcopies:
        c.start()
    for r in range(R):
        rows = rows_for(r, R)
        lo, hi = rows[0] * 3 * LAT, (rows[-1] + 1) * 3 * LAT
        for t in range(3):
            if lo:
                wpad[r, t * kpad : t * kpad + lo, :] = jnp.zeros((lo, C), BF16)
            if hi < kpad:
                wpad[r, t * kpad + hi : (t + 1) * kpad, :] = jnp.zeros((kpad - hi, C), BF16)
    def copy_to(d, o):
        return pltpu.make_async_remote_copy(
            src_ref=slots.at[0, b],
            dst_ref=slots.at[d, b],
            send_sem=send_sem.at[d, o],
            recv_sem=recv_sem.at[d, o],
            device_id={"block": k + d, "band": lax.rem(b + o, R)},
            device_id_type=MESH,
        )

    def pass_to(d, o, c):
        return pltpu.make_async_remote_copy(
            src_ref=slots.at[1, b],
            dst_ref=slots.at[d, b],
            send_sem=pass_sem.at[d, o, c],
            recv_sem=recv_sem.at[d, o],
            device_id={"block": k + d - 1, "band": lax.rem(b + o, R), "chan": c},
            device_id_type=MESH,
        )

    def copy_from(d, o):
        return pltpu.make_async_remote_copy(
            src_ref=slots.at[0, b],
            dst_ref=slots.at[d, lax.rem(b + R - o, R)],
            send_sem=send_sem.at[d, o],
            recv_sem=recv_sem.at[d, o],
            device_id={"block": k, "band": lax.rem(b + o, R)},
            device_id_type=MESH,
        )

    def sends(d):
        return k + d < nb if d < 2 else (k + d < nb) & odd

    def passes(d):
        return (k + d - 1 < nb) & passer

    a = lax.broadcasted_iota(jnp.int32, (R * 3 * 128, kpad), 0)
    c = lax.broadcasted_iota(jnp.int32, (R * 3 * 128, kpad), 1)
    sel = jnp.where(((a >> 7) * LAT + (a & (LAT - 1))) == c, 1.0, 0.0).astype(BF16)
    gmat = group_matrix(C, C)
    gmat2 = group_matrix(R * half, half)

    small[0].wait()
    peers = R - 1
    for d in range(1, reach + 1):
        peers = peers + jnp.where(sends(d), R, 0)
    for d in range(2, reach + 1):
        peers = peers + jnp.where(passes(d), R * (cores - 1), 0)
    pl.semaphore_wait(barrier, peers)
    for d in range(reach, -1, -1):
        @pl.when(sends(d))
        def _():
            for o in range(1 if d == 0 else 0, R):
                copy_to(d, o).start()

    @pl.when(passer)
    def _():
        copy_from(1, 0).wait_recv()
        for d in range(reach, 1, -1):
            @pl.when(passes(d))
            def _():
                for c in range(cores):
                    for o in range(R):
                        pass_to(d, o, c).start()

    small[1].wait()
    e = [jnp.int32(0)]
    for d in range(1, reach + 1):
        n = cnt_ref[jnp.maximum(k - d, 0)]
        e.append(e[-1] + jnp.where(k >= d, n, 0))
    before = e[-1]
    live = cnt_ref[k]

    def unpack(d):
        for r in range(R):
            xf[d * R + r] = slots[d, r].astype(F32)

    for o in range(1, R):
        copy_from(0, o).wait_recv()
    unpack(0)

    def earlier():
        for d in range(1, reach + 1):
            @pl.when((k >= d) & ~passer if d == 1 else k >= d)
            def _():
                copy_from(d, 0).wait_recv()
        for d in range(1, reach + 1):
            @pl.when(k >= d)
            def _():
                for o in range(1, R):
                    copy_from(d, o).wait_recv()
            unpack(d)

    W = COLS * LAT
    lane = lax.broadcasted_iota(jnp.int32, (8, W), 1)
    sub = lax.broadcasted_iota(jnp.int32, (8, W), 0)
    part = (lane >> 4) & 7
    mask = [part == ((sub + 7) & 7), part == sub, part == ((sub + 1) & 7)]
    zero128 = jnp.zeros((8, 128), F32)

    def expanded(j, r):
        if j >= 4:
            row = xf[r, j - 4 : j - 3, :]
        else:
            m = 4 - j
            d = jnp.int32(1)
            base = e[1]
            for q in range(1, reach):
                more = e[q] < m
                d = jnp.where(more, q + 1, d)
                base = jnp.where(more, e[q + 1], base)
            slot = jnp.clip(base - m, 0, SL - 1)
            row = xf[d * R + r, pl.ds(slot, 1), :]
            row = jnp.where(jnp.broadcast_to(before >= m, row.shape), row, 0.0)
        bc = jnp.broadcast_to(row, (8, W))
        prev = jnp.concatenate([zero128, bc[:, : W - 128]], axis=1)
        nxt = jnp.concatenate([bc[:, 128:], zero128], axis=1)
        ys = [
            jnp.where(mask[0], jnp.where(sub == 0, prev, bc), 0.0),
            jnp.where(mask[1], bc, 0.0),
            jnp.where(mask[2], jnp.where(sub == 7, nxt, bc), 0.0),
        ]
        return [
            jnp.concatenate([y[:, q * 128 : q * 128 + 128] for q in range(W // 128)], axis=0)
            for y in ys
        ]

    for p in reversed(range(FL // 2)):
        if p == 1:
            earlier()
        ex = {}
        for r in range(R):
            u, v = expanded(2 * p, r), expanded(2 * p + 1, r)
            ex[r] = [jnp.concatenate([u[x], v[x]], axis=0).astype(BF16) for x in range(3)]
        lhs = jnp.concatenate([ex[r][x] for r in range(R) for x in range(3)], axis=1)
        gf[p * 2 * COLS : (p + 1) * 2 * COLS, :] = jnp.dot(
            lhs, sel, preferred_element_type=F32
        )

    for c in wincopies:
        c.wait()
    MA = FA * COLS
    lhs = jnp.concatenate(
        [gf[t * COLS : t * COLS + MA, :] for t in range(3)], axis=1
    ).astype(BF16)
    rhs = jnp.concatenate([wpad[r] for r in range(R)], axis=1)
    y = jnp.dot(lhs, rhs, preferred_element_type=F32).astype(BF16).astype(F32)
    for r in range(R):
        c1s[r] = y[:, r * C : (r + 1) * C]

    s1, s2 = [], []
    for f in range(FA):
        a1 = a2 = None
        for r in range(R):
            h = c1s[r, f * COLS : (f + 1) * COLS, :]
            p1 = jnp.sum(h, axis=0, keepdims=True)
            p2 = jnp.sum(h * h, axis=0, keepdims=True)
            a1 = p1 if a1 is None else a1 + p1
            a2 = p2 if a2 is None else a2 + p2
        s1.append(a1)
        s2.append(a2)
    fill = jnp.zeros((16 - 2 * FA, C), F32)
    g = group_sums(jnp.concatenate(s1 + s2 + [fill], axis=0), gmat)
    total = float(R * COLS * GW)
    mean = g[:FA] / total
    var = g[FA : 2 * FA] / total - mean * mean
    inv = lax.rsqrt(var + EPSILON)
    for c in small[2:]:
        c.wait()
    scale = inv * (0.5 * gin_ref[...].reshape(1, C))
    shift = 0.5 * sin_ref[...].reshape(1, C) - mean * scale

    for r in range(R):
        act = []
        for f in range(FA):
            u = c1s[r, f * COLS : (f + 1) * COLS, :] * scale[f : f + 1] + shift[f : f + 1]
            a = silu_twice(u)
            if f < 2:
                a = jnp.where(jnp.broadcast_to(before >= 2 - f, a.shape), a, 0.0)
            act.append(a)
        for p in range(FA // 2):
            la[r, p * 2 * COLS : (p + 1) * 2 * COLS, :] = jnp.concatenate(
                act[2 * p : 2 * p + 2], axis=0
            ).astype(BF16)
        for p in range(SL // 2):
            lb[r, p * 2 * COLS : (p + 1) * 2 * COLS, :] = jnp.concatenate(
                act[2 * p + 1 : 2 * p + 3], axis=0
            ).astype(BF16)

    for c in wcopies:
        c.wait()
    M = SL * COLS
    wide = R * half
    lhs = []
    for t in range(3):
        for q in range(R):
            lhs.append(lb[q] if t == 1 else la[q, t * COLS : t * COLS + M, :])
    lhs = jnp.concatenate(lhs, axis=1)

    def taps(t, q, r, x):
        if 0 <= q - r + 1 <= 2:
            return wv[t, q - r + 1, x]
        return jnp.zeros((half, C), BF16)

    rhs = jnp.concatenate(
        [
            jnp.concatenate([taps(t, q, r, x) for t in range(3) for q in range(R)], axis=1)
            for x in range(3)
            for r in range(R)
        ],
        axis=0,
    )
    prod = lax.dot_general(lhs, rhs, (((1,), (1,)), ((), ())), preferred_element_type=F32)
    hs, t1, t2 = [], [], []
    col = lax.broadcasted_iota(jnp.int32, (COLS, wide), 0)
    for f in range(SL):
        p0, p1, p2 = [
            prod[f * COLS : (f + 1) * COLS, x * wide : (x + 1) * wide] for x in range(3)
        ]
        h = p1 + jnp.where(col == 0, 0.0, pltpu.roll(p0, 1, 0))
        h = h + jnp.where(col == COLS - 1, 0.0, pltpu.roll(p2, COLS - 1, 0))
        h = h.astype(BF16).astype(F32)
        hs.append(h)
        t1.append(jnp.sum(h, axis=0, keepdims=True))
        t2.append(jnp.sum(h * h, axis=0, keepdims=True))
    pad = jnp.zeros((16 - 2 * SL, wide), F32)
    g = group_sums(jnp.concatenate(t1 + t2 + [pad], axis=0), gmat2)
    mean = g[:SL] / total
    var = g[SL : 2 * SL] / total - mean * mean
    inv = lax.rsqrt(var + EPSILON)
    gains = jnp.concatenate([0.5 * gout_ref[...].reshape(1, half)] * R, axis=1)
    shifts = jnp.concatenate([0.5 * sout_ref[...].reshape(1, half)] * R, axis=1)
    scale = inv * gains
    shift = shifts - mean * scale
    for r in range(R):
        lo = r * half // 128 * 128
        hi = min(up((r + 1) * half, 128), wide)

        @pl.when(b == r)
        def _():
            for f in range(SL):
                u = hs[f][:, lo:hi] * scale[f : f + 1, lo:hi] + shift[f : f + 1, lo:hi]
                a = silu_twice(u)
                a = jnp.where(jnp.broadcast_to(f < live, a.shape), a, 0.0)
                out_ref[f] = a.T[r * half - lo : (r + 1) * half - lo].astype(BF16)

    for o in range(1, R):
        copy_to(0, o).wait_send()
    for d in range(1, reach + 1):
        @pl.when(sends(d))
        def _():
            for o in range(R):
                copy_to(d, o).wait_send()
    for d in range(2, reach + 1):
        @pl.when(passes(d))
        def _():
            for c in range(cores):
                for o in range(R):
                    pass_to(d, o, c).wait_send()


def shards(latents, frame_counts, w_in, gain_in, shift_in, w_mid, gain_out, shift_out):
    SL, band_rows, width = latents.shape
    COLS = width // LAT
    half = w_mid.shape[4]
    R = lax.axis_size("band") * band_rows
    nb = lax.axis_size("block")
    cores = lax.axis_size("chan")
    reach = min(4, nb - 1)
    FL, FA = SL + 4, SL + 2
    kpad = up(R * 3 * LAT, 128)
    vmem = pl.BlockSpec(memory_space=pltpu.VMEM)
    hbm = pl.BlockSpec(memory_space=pltpu.HBM)
    raw = pl.pallas_call(
        functools.partial(body, nb, R, COLS, SL, reach),
        out_shape=pltpu.VMEM((SL, half, COLS), BF16),
        in_specs=[hbm] * 8,
        out_specs=vmem,
        scratch_shapes=[
            pltpu.SMEM(frame_counts.shape, jnp.int32),
            pltpu.VMEM((C,), F32),
            pltpu.VMEM((C,), F32),
            pltpu.VMEM((half,), F32),
            pltpu.VMEM((half,), F32),
            pltpu.VMEM((reach + 1, R, SL, width), BF16),
            pltpu.VMEM(((reach + 1) * R, SL, width), F32),
            pltpu.VMEM((FL * COLS, kpad), F32),
            pltpu.VMEM((R, 3 * kpad, C), BF16),
            pltpu.VMEM((R, FA * COLS, C), F32),
            pltpu.VMEM((R, FA * COLS, C), BF16),
            pltpu.VMEM((R, SL * COLS, C), BF16),
            pltpu.VMEM((3, 3, 3, half, C), BF16),
            pltpu.SemaphoreType.DMA((reach + 1, R)),
            pltpu.SemaphoreType.DMA((reach + 1, R, cores)),
            pltpu.SemaphoreType.DMA((reach + 1, R)),
            pltpu.SemaphoreType.DMA((3,)),
            pltpu.SemaphoreType.DMA((R, 3)),
            pltpu.SemaphoreType.DMA((6,)),
        ],
        compiler_params=pltpu.CompilerParams(
            collective_id=0, has_side_effects=True, vmem_limit_bytes=40 * 1024 * 1024
        ),
    )(*[pltpu.with_memory_space_constraint(z, pltpu.HBM) for z in (
        frame_counts,
        latents.reshape(SL, width),
        w_in.reshape(3, 9 * LAT, C),
        gain_in,
        shift_in,
        jnp.swapaxes(w_mid, 3, 4),
        gain_out,
        shift_out,
    )])
    return jnp.swapaxes(raw, 1, 2)[:, None]


def solution(mesh):
    return jax.shard_map(
        shards,
        mesh=mesh,
        in_specs=(
            P(("video", "block"), "band", None),
            P("video"),
            P(),
            P(),
            P(),
            P(None, None, None, None, "chan"),
            P("chan"),
            P("chan"),
        ),
        out_specs=P(("video", "block"), "band", None, "chan"),
        check_vma=False,
    )
```

```python
import functools

import jax
import jax.numpy as jnp
from jax import lax
from jax.experimental import pallas as pl
from jax.experimental.pallas import tpu as pltpu
from jax.sharding import PartitionSpec as P

LAT = 16
C = 384
GROUPS = 32
GW = C // GROUPS
EPSILON = 1e-06
MESH = pl.DeviceIdType.MESH
F32 = jnp.float32
BF16 = jnp.bfloat16


def up(n, m):
    return (n + m - 1) // m * m


def rows_for(r, R):
    return tuple(range(max(0, r - 1), min(R - 1, r + 1) + 1))


def group_matrix(n, width):
    a = lax.broadcasted_iota(jnp.int32, (n, n), 0)
    b = lax.broadcasted_iota(jnp.int32, (n, n), 1)
    for q in range(n // width - 1, 0, -1):
        a = jnp.where(a >= q * width, a - q * width, a)
        b = jnp.where(b >= q * width, b - q * width, b)
    same = ((a * 5462) >> 16) == ((b * 5462) >> 16)
    return jnp.where(same, 1.0, 0.0).astype(BF16)


def group_sums(x, gmat):
    hi = x.astype(BF16)
    rest = x - hi.astype(F32)
    mid = rest.astype(BF16)
    lo = (rest - mid.astype(F32)).astype(BF16)
    n = x.shape[0]
    y = jnp.dot(
        jnp.concatenate([hi, mid, lo], axis=0), gmat, preferred_element_type=F32
    )
    return y[:n] + y[n : 2 * n] + y[2 * n :]


def silu_twice(v):
    return v + v * jnp.tanh(v)


def body(
    nb, R, COLS, SL, reach,
    cnt_hbm, lat_ref, win_ref, gin_hbm, sin_hbm, wmid_ref, gout_hbm, sout_hbm,
    out_ref,
    cnt_ref, gin_ref, sin_ref, gout_ref, sout_ref,
    slots, xf, gf, wpad, c1s, la, lb, wv,
    send_sem, pass_sem, recv_sem, w_sem, win_sem, in_sem,
):
    k = lax.axis_index("block")
    b = lax.axis_index("band")
    half = out_ref.shape[1]
    FL = SL + 4
    FA = SL + 2

    wcopies = []
    for t in range(3):
        c = pltpu.make_async_copy(
            wmid_ref.at[t], wv.at[t], w_sem.at[t]
        )
        wcopies.append(c)
    wincopies = []
    kpad = wpad.shape[1] // 3
    for r in range(R):
        rows = rows_for(r, R)
        first = (rows[0] - r + 1) * 3 * LAT
        size = len(rows) * 3 * LAT
        for t in range(3):
            c = pltpu.make_async_copy(
                win_ref.at[t, pl.ds(first, size)],
                wpad.at[r, pl.ds(t * kpad + rows[0] * 3 * LAT, size)],
                win_sem.at[r, t],
            )
            wincopies.append(c)
    barrier = pltpu.get_barrier_semaphore()
    odd = lax.rem(k, 2) == 1
    for d in range(reach + 1):
        from_there = k >= d if d < 2 else (k >= d) & (lax.rem(k + d, 2) == 1)
        @pl.when(from_there)
        def _():
            for o in range(1 if d == 0 else 0, R):
                pl.semaphore_signal(
                    barrier, inc=1,
                    device_id={"block": k - d, "band": lax.rem(b + R - o, R)},
                    device_id_type=MESH,
                )
    small = [
        pltpu.make_async_copy(src, dst, in_sem.at[i])
        for i, (src, dst) in enumerate(
            [
                (lat_ref, slots.at[0, b]), (cnt_hbm, cnt_ref), (gin_hbm, gin_ref),
                (sin_hbm, sin_ref), (gout_hbm, gout_ref), (sout_hbm, sout_ref),
            ]
        )
    ]
    for c in small + wincopies + wcopies:
        c.start()
    for r in range(R):
        rows = rows_for(r, R)
        lo, hi = rows[0] * 3 * LAT, (rows[-1] + 1) * 3 * LAT
        for t in range(3):
            if lo:
                wpad[r, t * kpad : t * kpad + lo, :] = jnp.zeros((lo, C), BF16)
            if hi < kpad:
                wpad[r, t * kpad + hi : (t + 1) * kpad, :] = jnp.zeros((kpad - hi, C), BF16)
    def copy_to(d, o, passed=False):
        return pltpu.make_async_remote_copy(
            src_ref=slots.at[1 if passed else 0, b],
            dst_ref=slots.at[d, b],
            send_sem=(pass_sem if passed else send_sem).at[d, o],
            recv_sem=recv_sem.at[d, o],
            device_id={"block": k + d - (1 if passed else 0), "band": lax.rem(b + o, R)},
            device_id_type=MESH,
        )

    def copy_from(d, o):
        return pltpu.make_async_remote_copy(
            src_ref=slots.at[0, b],
            dst_ref=slots.at[d, lax.rem(b + R - o, R)],
            send_sem=send_sem.at[d, o],
            recv_sem=recv_sem.at[d, o],
            device_id={"block": k, "band": lax.rem(b + o, R)},
            device_id_type=MESH,
        )

    def sends(d):
        return k + d < nb if d < 2 else (k + d < nb) & odd

    def passes(d):
        return (k + d - 1 < nb) & odd

    a = lax.broadcasted_iota(jnp.int32, (R * 3 * 128, kpad), 0)
    c = lax.broadcasted_iota(jnp.int32, (R * 3 * 128, kpad), 1)
    sel = jnp.where(((a >> 7) * LAT + (a & (LAT - 1))) == c, 1.0, 0.0).astype(BF16)
    gmat = group_matrix(C, C)
    gmat2 = group_matrix(R * half, half)

    small[0].wait()
    peers = R - 1
    for d in range(1, reach + 1):
        peers = peers + jnp.where(sends(d), R, 0)
    pl.semaphore_wait(barrier, peers)
    for d in range(reach, -1, -1):
        @pl.when(sends(d))
        def _():
            for o in range(1 if d == 0 else 0, R):
                copy_to(d, o).start()

    @pl.when(odd)
    def _():
        copy_from(1, 0).wait_recv()
        for d in range(2, reach + 1):
            @pl.when(passes(d))
            def _():
                for o in range(R):
                    copy_to(d, o, True).start()

    small[1].wait()
    e = [jnp.int32(0)]
    for d in range(1, reach + 1):
        n = cnt_ref[jnp.maximum(k - d, 0)]
        e.append(e[-1] + jnp.where(k >= d, n, 0))
    before = e[-1]
    live = cnt_ref[k]

    def unpack(d):
        for r in range(R):
            xf[d * R + r] = slots[d, r].astype(F32)

    for o in range(1, R):
        copy_from(0, o).wait_recv()
    unpack(0)

    def earlier():
        for d in range(1, reach + 1):
            @pl.when((k >= d) & ~odd if d == 1 else k >= d)
            def _():
                copy_from(d, 0).wait_recv()
        for d in range(1, reach + 1):
            @pl.when(k >= d)
            def _():
                for o in range(1, R):
                    copy_from(d, o).wait_recv()
            unpack(d)

    W = COLS * LAT
    lane = lax.broadcasted_iota(jnp.int32, (8, W), 1)
    sub = lax.broadcasted_iota(jnp.int32, (8, W), 0)
    part = (lane >> 4) & 7
    mask = [part == ((sub + 7) & 7), part == sub, part == ((sub + 1) & 7)]
    zero128 = jnp.zeros((8, 128), F32)

    def expanded(j, r):
        if j >= 4:
            row = xf[r, j - 4 : j - 3, :]
        else:
            m = 4 - j
            d = jnp.int32(1)
            base = e[1]
            for q in range(1, reach):
                more = e[q] < m
                d = jnp.where(more, q + 1, d)
                base = jnp.where(more, e[q + 1], base)
            slot = jnp.clip(base - m, 0, SL - 1)
            row = xf[d * R + r, pl.ds(slot, 1), :]
            row = jnp.where(jnp.broadcast_to(before >= m, row.shape), row, 0.0)
        bc = jnp.broadcast_to(row, (8, W))
        prev = jnp.concatenate([zero128, bc[:, : W - 128]], axis=1)
        nxt = jnp.concatenate([bc[:, 128:], zero128], axis=1)
        ys = [
            jnp.where(mask[0], jnp.where(sub == 0, prev, bc), 0.0),
            jnp.where(mask[1], bc, 0.0),
            jnp.where(mask[2], jnp.where(sub == 7, nxt, bc), 0.0),
        ]
        return [
            jnp.concatenate([y[:, q * 128 : q * 128 + 128] for q in range(W // 128)], axis=0)
            for y in ys
        ]

    def expand_pairs(pairs):
        for p in pairs:
            ex = {}
            for r in range(R):
                u, v = expanded(2 * p, r), expanded(2 * p + 1, r)
                ex[r] = [jnp.concatenate([u[x], v[x]], axis=0).astype(BF16) for x in range(3)]
            lhs = jnp.concatenate([ex[r][x] for r in range(R) for x in range(3)], axis=1)
            gf[p * 2 * COLS : (p + 1) * 2 * COLS, :] = jnp.dot(
                lhs, sel, preferred_element_type=F32
            )

    total = float(R * COLS * GW)
    act = {}

    def first_stage(lo, hi):
        n = hi - lo
        lhs = jnp.concatenate(
            [gf[(lo + t) * COLS : (hi + t) * COLS, :] for t in range(3)], axis=1
        ).astype(BF16)
        rhs = jnp.concatenate([wpad[r] for r in range(R)], axis=1)
        y = jnp.dot(lhs, rhs, preferred_element_type=F32).astype(BF16).astype(F32)
        for r in range(R):
            c1s[r, lo * COLS : hi * COLS, :] = y[:, r * C : (r + 1) * C]
        s1, s2 = [], []
        for f in range(lo, hi):
            a1 = a2 = None
            for r in range(R):
                h = c1s[r, f * COLS : (f + 1) * COLS, :]
                p1 = jnp.sum(h, axis=0, keepdims=True)
                p2 = jnp.sum(h * h, axis=0, keepdims=True)
                a1 = p1 if a1 is None else a1 + p1
                a2 = p2 if a2 is None else a2 + p2
            s1.append(a1)
            s2.append(a2)
        fill = [jnp.zeros((16 - 2 * n, C), F32)] if n < 8 else []
        g = group_sums(jnp.concatenate(s1 + s2 + fill, axis=0), gmat)
        mean = g[:n] / total
        var = g[n : 2 * n] / total - mean * mean
        inv = lax.rsqrt(var + EPSILON)
        scale = inv * (0.5 * gin_ref[...].reshape(1, C))
        shift = 0.5 * sin_ref[...].reshape(1, C) - mean * scale
        for r in range(R):
            for f in range(lo, hi):
                q = f - lo
                u = c1s[r, f * COLS : (f + 1) * COLS, :] * scale[q : q + 1] + shift[q : q + 1]
                a = silu_twice(u)
                if f < 2:
                    a = jnp.where(jnp.broadcast_to(before >= 2 - f, a.shape), a, 0.0)
                act[r, f] = a

    def store_pair(ref, at, r, f):
        ref[r, at * 2 * COLS : (at + 1) * 2 * COLS, :] = jnp.concatenate(
            [act[r, f], act[r, f + 1]], axis=0
        ).astype(BF16)

    expand_pairs(reversed(range(2, FL // 2)))
    for c in wincopies + small[2:]:
        c.wait()
    first_stage(4, FA)
    earlier()
    expand_pairs((1, 0))
    first_stage(0, 4)
    for r in range(R):
        for p in range(FA // 2):
            store_pair(la, p, r, 2 * p)
        for p in range(SL // 2):
            store_pair(lb, p, r, 2 * p + 1)

    for c in wcopies:
        c.wait()
    M = SL * COLS
    wide = R * half
    lhs = []
    for t in range(3):
        for q in range(R):
            lhs.append(lb[q] if t == 1 else la[q, t * COLS : t * COLS + M, :])
    lhs = jnp.concatenate(lhs, axis=1)

    def taps(t, q, r, x):
        if 0 <= q - r + 1 <= 2:
            return wv[t, q - r + 1, x]
        return jnp.zeros((half, C), BF16)

    rhs = jnp.concatenate(
        [
            jnp.concatenate([taps(t, q, r, x) for t in range(3) for q in range(R)], axis=1)
            for x in range(3)
            for r in range(R)
        ],
        axis=0,
    )
    prod = lax.dot_general(lhs, rhs, (((1,), (1,)), ((), ())), preferred_element_type=F32)
    hs, t1, t2 = [], [], []
    col = lax.broadcasted_iota(jnp.int32, (COLS, wide), 0)
    for f in range(SL):
        p0, p1, p2 = [
            prod[f * COLS : (f + 1) * COLS, x * wide : (x + 1) * wide] for x in range(3)
        ]
        h = p1 + jnp.where(col == 0, 0.0, pltpu.roll(p0, 1, 0))
        h = h + jnp.where(col == COLS - 1, 0.0, pltpu.roll(p2, COLS - 1, 0))
        h = h.astype(BF16).astype(F32)
        hs.append(h)
        t1.append(jnp.sum(h, axis=0, keepdims=True))
        t2.append(jnp.sum(h * h, axis=0, keepdims=True))
    pad = jnp.zeros((16 - 2 * SL, wide), F32)
    g = group_sums(jnp.concatenate(t1 + t2 + [pad], axis=0), gmat2)
    mean = g[:SL] / total
    var = g[SL : 2 * SL] / total - mean * mean
    inv = lax.rsqrt(var + EPSILON)
    gains = jnp.concatenate([0.5 * gout_ref[...].reshape(1, half)] * R, axis=1)
    shifts = jnp.concatenate([0.5 * sout_ref[...].reshape(1, half)] * R, axis=1)
    scale = inv * gains
    shift = shifts - mean * scale
    for r in range(R):
        lo = r * half // 128 * 128
        hi = min(up((r + 1) * half, 128), wide)

        @pl.when(b == r)
        def _():
            for f in range(SL):
                u = hs[f][:, lo:hi] * scale[f : f + 1, lo:hi] + shift[f : f + 1, lo:hi]
                a = silu_twice(u)
                a = jnp.where(jnp.broadcast_to(f < live, a.shape), a, 0.0)
                out_ref[f] = a.T[r * half - lo : (r + 1) * half - lo].astype(BF16)

    for o in range(1, R):
        copy_to(0, o).wait_send()
    for d in range(1, reach + 1):
        @pl.when(sends(d))
        def _():
            for o in range(R):
                copy_to(d, o).wait_send()
    for d in range(2, reach + 1):
        @pl.when(passes(d))
        def _():
            for o in range(R):
                copy_to(d, o, True).wait_send()


def shards(latents, frame_counts, w_in, gain_in, shift_in, w_mid, gain_out, shift_out):
    SL, band_rows, width = latents.shape
    COLS = width // LAT
    half = w_mid.shape[4]
    R = lax.axis_size("band") * band_rows
    nb = lax.axis_size("block")
    reach = min(4, nb - 1)
    FL, FA = SL + 4, SL + 2
    kpad = up(R * 3 * LAT, 128)
    vmem = pl.BlockSpec(memory_space=pltpu.VMEM)
    hbm = pl.BlockSpec(memory_space=pltpu.HBM)
    raw = pl.pallas_call(
        functools.partial(body, nb, R, COLS, SL, reach),
        out_shape=pltpu.VMEM((SL, half, COLS), BF16),
        in_specs=[hbm] * 8,
        out_specs=vmem,
        scratch_shapes=[
            pltpu.SMEM(frame_counts.shape, jnp.int32),
            pltpu.VMEM((C,), F32),
            pltpu.VMEM((C,), F32),
            pltpu.VMEM((half,), F32),
            pltpu.VMEM((half,), F32),
            pltpu.VMEM((reach + 1, R, SL, width), BF16),
            pltpu.VMEM(((reach + 1) * R, SL, width), F32),
            pltpu.VMEM((FL * COLS, kpad), F32),
            pltpu.VMEM((R, 3 * kpad, C), BF16),
            pltpu.VMEM((R, FA * COLS, C), F32),
            pltpu.VMEM((R, FA * COLS, C), BF16),
            pltpu.VMEM((R, SL * COLS, C), BF16),
            pltpu.VMEM((3, 3, 3, half, C), BF16),
            pltpu.SemaphoreType.DMA((reach + 1, R)),
            pltpu.SemaphoreType.DMA((reach + 1, R)),
            pltpu.SemaphoreType.DMA((reach + 1, R)),
            pltpu.SemaphoreType.DMA((3,)),
            pltpu.SemaphoreType.DMA((R, 3)),
            pltpu.SemaphoreType.DMA((6,)),
        ],
        compiler_params=pltpu.CompilerParams(
            collective_id=0, has_side_effects=True, vmem_limit_bytes=40 * 1024 * 1024
        ),
    )(*[pltpu.with_memory_space_constraint(z, pltpu.HBM) for z in (
        frame_counts,
        latents.reshape(SL, width),
        w_in.reshape(3, 9 * LAT, C),
        gain_in,
        shift_in,
        jnp.swapaxes(w_mid, 3, 4),
        gain_out,
        shift_out,
    )])
    return jnp.swapaxes(raw, 1, 2)[:, None]


def solution(mesh):
    return jax.shard_map(
        shards,
        mesh=mesh,
        in_specs=(
            P(("video", "block"), "band", None),
            P("video"),
            P(),
            P(),
            P(),
            P(None, None, None, None, "chan"),
            P("chan"),
            P("chan"),
        ),
        out_specs=P(("video", "block"), "band", None, "chan"),
        check_vma=False,
    )
```

```python
import functools

import jax
import jax.numpy as jnp
from jax import lax
from jax.experimental import pallas as pl
from jax.experimental.pallas import tpu as pltpu
from jax.sharding import PartitionSpec as P

LAT = 16
C = 384
GROUPS = 32
GW = C // GROUPS
EPSILON = 1e-06
MESH = pl.DeviceIdType.MESH
F32 = jnp.float32
BF16 = jnp.bfloat16


def up(n, m):
    return (n + m - 1) // m * m


def rows_for(r, R):
    return tuple(range(max(0, r - 1), min(R - 1, r + 1) + 1))


def group_matrix(n, width):
    a = lax.broadcasted_iota(jnp.int32, (n, n), 0)
    b = lax.broadcasted_iota(jnp.int32, (n, n), 1)
    for q in range(n // width - 1, 0, -1):
        a = jnp.where(a >= q * width, a - q * width, a)
        b = jnp.where(b >= q * width, b - q * width, b)
    same = ((a * 5462) >> 16) == ((b * 5462) >> 16)
    return jnp.where(same, 1.0, 0.0).astype(BF16)


def group_sums(x, gmat):
    hi = x.astype(BF16)
    rest = x - hi.astype(F32)
    mid = rest.astype(BF16)
    lo = (rest - mid.astype(F32)).astype(BF16)
    n = x.shape[0]
    y = jnp.dot(
        jnp.concatenate([hi, mid, lo], axis=0), gmat, preferred_element_type=F32
    )
    return y[:n] + y[n : 2 * n] + y[2 * n :]


def silu_twice(v):
    return v + v * jnp.tanh(v)


def body(
    nb, R, COLS, SL, reach,
    cnt_hbm, lat_ref, win_ref, gin_hbm, sin_hbm, wmid_ref, gout_hbm, sout_hbm,
    out_ref,
    cnt_ref, gin_ref, sin_ref, gout_ref, sout_ref,
    slots, xf, gf, wpad, c1s, la, lb, wv,
    send_sem, pass_sem, recv_sem, w_sem, win_sem, in_sem,
):
    k = lax.axis_index("block")
    b = lax.axis_index("band")
    half = out_ref.shape[1]
    FL = SL + 4
    FA = SL + 2

    wcopies = []
    for t in range(3):
        c = pltpu.make_async_copy(
            wmid_ref.at[t], wv.at[t], w_sem.at[t]
        )
        wcopies.append(c)
    wincopies = []
    kpad = wpad.shape[1] // 3
    for r in range(R):
        rows = rows_for(r, R)
        first = (rows[0] - r + 1) * 3 * LAT
        size = len(rows) * 3 * LAT
        for t in range(3):
            c = pltpu.make_async_copy(
                win_ref.at[t, pl.ds(first, size)],
                wpad.at[r, pl.ds(t * kpad + rows[0] * 3 * LAT, size)],
                win_sem.at[r, t],
            )
            wincopies.append(c)
    barrier = pltpu.get_barrier_semaphore()
    odd = lax.rem(k, 2) == 1
    for d in range(reach + 1):
        from_there = k >= d if d < 2 else (k >= d) & (lax.rem(k + d, 2) == 1)
        @pl.when(from_there)
        def _():
            for o in range(1 if d == 0 else 0, R):
                pl.semaphore_signal(
                    barrier, inc=1,
                    device_id={"block": k - d, "band": lax.rem(b + R - o, R)},
                    device_id_type=MESH,
                )
    small = [
        pltpu.make_async_copy(src, dst, in_sem.at[i])
        for i, (src, dst) in enumerate(
            [
                (lat_ref, slots.at[0, b]), (cnt_hbm, cnt_ref), (gin_hbm, gin_ref),
                (sin_hbm, sin_ref), (gout_hbm, gout_ref), (sout_hbm, sout_ref),
            ]
        )
    ]
    for c in small + wincopies + wcopies:
        c.start()
    for r in range(R):
        rows = rows_for(r, R)
        lo, hi = rows[0] * 3 * LAT, (rows[-1] + 1) * 3 * LAT
        for t in range(3):
            if lo:
                wpad[r, t * kpad : t * kpad + lo, :] = jnp.zeros((lo, C), BF16)
            if hi < kpad:
                wpad[r, t * kpad + hi : (t + 1) * kpad, :] = jnp.zeros((kpad - hi, C), BF16)
    def copy_to(d, o, passed=False):
        return pltpu.make_async_remote_copy(
            src_ref=slots.at[1 if passed else 0, b],
            dst_ref=slots.at[d, b],
            send_sem=(pass_sem if passed else send_sem).at[d, o],
            recv_sem=recv_sem.at[d, o],
            device_id={"block": k + d - (1 if passed else 0), "band": lax.rem(b + o, R)},
            device_id_type=MESH,
        )

    def copy_from(d, o):
        return pltpu.make_async_remote_copy(
            src_ref=slots.at[0, b],
            dst_ref=slots.at[d, lax.rem(b + R - o, R)],
            send_sem=send_sem.at[d, o],
            recv_sem=recv_sem.at[d, o],
            device_id={"block": k, "band": lax.rem(b + o, R)},
            device_id_type=MESH,
        )

    def sends(d):
        return k + d < nb if d < 2 else (k + d < nb) & odd

    def passes(d):
        return (k + d - 1 < nb) & odd

    a = lax.broadcasted_iota(jnp.int32, (R * 3 * 128, kpad), 0)
    c = lax.broadcasted_iota(jnp.int32, (R * 3 * 128, kpad), 1)
    sel = jnp.where(((a >> 7) * LAT + (a & (LAT - 1))) == c, 1.0, 0.0).astype(BF16)
    gmat = group_matrix(C, C)
    gmat2 = group_matrix(R * half, half)

    small[0].wait()
    peers = R - 1
    for d in range(1, reach + 1):
        peers = peers + jnp.where(sends(d), R, 0)
    pl.semaphore_wait(barrier, peers)
    for d in range(reach + 1):
        @pl.when(sends(d))
        def _():
            for o in range(1 if d == 0 else 0, R):
                copy_to(d, o).start()

    @pl.when(odd)
    def _():
        copy_from(1, 0).wait_recv()
        for d in range(2, reach + 1):
            @pl.when(passes(d))
            def _():
                for o in range(R):
                    copy_to(d, o, True).start()

    small[1].wait()
    e = [jnp.int32(0)]
    for d in range(1, reach + 1):
        n = cnt_ref[jnp.maximum(k - d, 0)]
        e.append(e[-1] + jnp.where(k >= d, n, 0))
    before = e[-1]
    live = cnt_ref[k]

    def unpack(d):
        for r in range(R):
            xf[d * R + r] = slots[d, r].astype(F32)

    for o in range(1, R):
        copy_from(0, o).wait_recv()
    unpack(0)

    def earlier():
        for d in range(1, reach + 1):
            @pl.when((k >= d) & ~odd if d == 1 else k >= d)
            def _():
                copy_from(d, 0).wait_recv()
        for d in range(1, reach + 1):
            @pl.when(k >= d)
            def _():
                for o in range(1, R):
                    copy_from(d, o).wait_recv()
            unpack(d)

    W = COLS * LAT
    lane = lax.broadcasted_iota(jnp.int32, (8, W), 1)
    sub = lax.broadcasted_iota(jnp.int32, (8, W), 0)
    part = (lane >> 4) & 7
    mask = [part == ((sub + 7) & 7), part == sub, part == ((sub + 1) & 7)]
    zero128 = jnp.zeros((8, 128), F32)

    def expanded(j, r):
        if j >= 4:
            row = xf[r, j - 4 : j - 3, :]
        else:
            m = 4 - j
            d = jnp.int32(1)
            base = e[1]
            for q in range(1, reach):
                more = e[q] < m
                d = jnp.where(more, q + 1, d)
                base = jnp.where(more, e[q + 1], base)
            slot = jnp.clip(base - m, 0, SL - 1)
            row = xf[d * R + r, pl.ds(slot, 1), :]
            row = jnp.where(jnp.broadcast_to(before >= m, row.shape), row, 0.0)
        bc = jnp.broadcast_to(row, (8, W))
        prev = jnp.concatenate([zero128, bc[:, : W - 128]], axis=1)
        nxt = jnp.concatenate([bc[:, 128:], zero128], axis=1)
        ys = [
            jnp.where(mask[0], jnp.where(sub == 0, prev, bc), 0.0),
            jnp.where(mask[1], bc, 0.0),
            jnp.where(mask[2], jnp.where(sub == 7, nxt, bc), 0.0),
        ]
        return [
            jnp.concatenate([y[:, q * 128 : q * 128 + 128] for q in range(W // 128)], axis=0)
            for y in ys
        ]

    def expand_pairs(pairs):
        for p in pairs:
            ex = {}
            for r in range(R):
                u, v = expanded(2 * p, r), expanded(2 * p + 1, r)
                ex[r] = [jnp.concatenate([u[x], v[x]], axis=0).astype(BF16) for x in range(3)]
            lhs = jnp.concatenate([ex[r][x] for r in range(R) for x in range(3)], axis=1)
            gf[p * 2 * COLS : (p + 1) * 2 * COLS, :] = jnp.dot(
                lhs, sel, preferred_element_type=F32
            )

    total = float(R * COLS * GW)
    act = {}

    def first_stage(lo, hi):
        n = hi - lo
        lhs = jnp.concatenate(
            [gf[(lo + t) * COLS : (hi + t) * COLS, :] for t in range(3)], axis=1
        ).astype(BF16)
        rhs = jnp.concatenate([wpad[r] for r in range(R)], axis=1)
        y = jnp.dot(lhs, rhs, preferred_element_type=F32).astype(BF16).astype(F32)
        for r in range(R):
            c1s[r, lo * COLS : hi * COLS, :] = y[:, r * C : (r + 1) * C]
        s1, s2 = [], []
        for f in range(lo, hi):
            a1 = a2 = None
            for r in range(R):
                h = c1s[r, f * COLS : (f + 1) * COLS, :]
                p1 = jnp.sum(h, axis=0, keepdims=True)
                p2 = jnp.sum(h * h, axis=0, keepdims=True)
                a1 = p1 if a1 is None else a1 + p1
                a2 = p2 if a2 is None else a2 + p2
            s1.append(a1)
            s2.append(a2)
        fill = [jnp.zeros((16 - 2 * n, C), F32)] if n < 8 else []
        g = group_sums(jnp.concatenate(s1 + s2 + fill, axis=0), gmat)
        mean = g[:n] / total
        var = g[n : 2 * n] / total - mean * mean
        inv = lax.rsqrt(var + EPSILON)
        scale = inv * (0.5 * gin_ref[...].reshape(1, C))
        shift = 0.5 * sin_ref[...].reshape(1, C) - mean * scale
        for r in range(R):
            for f in range(lo, hi):
                q = f - lo
                u = c1s[r, f * COLS : (f + 1) * COLS, :] * scale[q : q + 1] + shift[q : q + 1]
                a = silu_twice(u)
                if f < 2:
                    a = jnp.where(jnp.broadcast_to(before >= 2 - f, a.shape), a, 0.0)
                act[r, f] = a

    def store_pair(ref, at, r, f):
        ref[r, at * 2 * COLS : (at + 1) * 2 * COLS, :] = jnp.concatenate(
            [act[r, f], act[r, f + 1]], axis=0
        ).astype(BF16)

    expand_pairs(reversed(range(2, FL // 2)))
    for c in wincopies + small[2:]:
        c.wait()
    first_stage(4, FA)
    earlier()
    expand_pairs((1, 0))
    first_stage(0, 4)
    for r in range(R):
        for p in range(FA // 2):
            store_pair(la, p, r, 2 * p)
        for p in range(SL // 2):
            store_pair(lb, p, r, 2 * p + 1)

    for c in wcopies:
        c.wait()
    M = SL * COLS
    wide = R * half
    lhs = []
    for t in range(3):
        for q in range(R):
            lhs.append(lb[q] if t == 1 else la[q, t * COLS : t * COLS + M, :])
    lhs = jnp.concatenate(lhs, axis=1)

    def taps(t, q, r, x):
        if 0 <= q - r + 1 <= 2:
            return wv[t, q - r + 1, x]
        return jnp.zeros((half, C), BF16)

    rhs = jnp.concatenate(
        [
            jnp.concatenate([taps(t, q, r, x) for t in range(3) for q in range(R)], axis=1)
            for x in range(3)
            for r in range(R)
        ],
        axis=0,
    )
    prod = lax.dot_general(lhs, rhs, (((1,), (1,)), ((), ())), preferred_element_type=F32)
    hs, t1, t2 = [], [], []
    col = lax.broadcasted_iota(jnp.int32, (COLS, wide), 0)
    for f in range(SL):
        p0, p1, p2 = [
            prod[f * COLS : (f + 1) * COLS, x * wide : (x + 1) * wide] for x in range(3)
        ]
        h = p1 + jnp.where(col == 0, 0.0, pltpu.roll(p0, 1, 0))
        h = h + jnp.where(col == COLS - 1, 0.0, pltpu.roll(p2, COLS - 1, 0))
        h = h.astype(BF16).astype(F32)
        hs.append(h)
        t1.append(jnp.sum(h, axis=0, keepdims=True))
        t2.append(jnp.sum(h * h, axis=0, keepdims=True))
    pad = jnp.zeros((16 - 2 * SL, wide), F32)
    g = group_sums(jnp.concatenate(t1 + t2 + [pad], axis=0), gmat2)
    mean = g[:SL] / total
    var = g[SL : 2 * SL] / total - mean * mean
    inv = lax.rsqrt(var + EPSILON)
    gains = jnp.concatenate([0.5 * gout_ref[...].reshape(1, half)] * R, axis=1)
    shifts = jnp.concatenate([0.5 * sout_ref[...].reshape(1, half)] * R, axis=1)
    scale = inv * gains
    shift = shifts - mean * scale
    for r in range(R):
        lo = r * half // 128 * 128
        hi = min(up((r + 1) * half, 128), wide)

        @pl.when(b == r)
        def _():
            for f in range(SL):
                u = hs[f][:, lo:hi] * scale[f : f + 1, lo:hi] + shift[f : f + 1, lo:hi]
                a = silu_twice(u)
                a = jnp.where(jnp.broadcast_to(f < live, a.shape), a, 0.0)
                out_ref[f] = a.T[r * half - lo : (r + 1) * half - lo].astype(BF16)

    for o in range(1, R):
        copy_to(0, o).wait_send()
    for d in range(1, reach + 1):
        @pl.when(sends(d))
        def _():
            for o in range(R):
                copy_to(d, o).wait_send()
    for d in range(2, reach + 1):
        @pl.when(passes(d))
        def _():
            for o in range(R):
                copy_to(d, o, True).wait_send()


def shards(latents, frame_counts, w_in, gain_in, shift_in, w_mid, gain_out, shift_out):
    SL, band_rows, width = latents.shape
    COLS = width // LAT
    half = w_mid.shape[4]
    R = lax.axis_size("band") * band_rows
    nb = lax.axis_size("block")
    reach = min(4, nb - 1)
    FL, FA = SL + 4, SL + 2
    kpad = up(R * 3 * LAT, 128)
    vmem = pl.BlockSpec(memory_space=pltpu.VMEM)
    hbm = pl.BlockSpec(memory_space=pltpu.HBM)
    raw = pl.pallas_call(
        functools.partial(body, nb, R, COLS, SL, reach),
        out_shape=pltpu.VMEM((SL, half, COLS), BF16),
        in_specs=[hbm] * 8,
        out_specs=vmem,
        scratch_shapes=[
            pltpu.SMEM(frame_counts.shape, jnp.int32),
            pltpu.VMEM((C,), F32),
            pltpu.VMEM((C,), F32),
            pltpu.VMEM((half,), F32),
            pltpu.VMEM((half,), F32),
            pltpu.VMEM((reach + 1, R, SL, width), BF16),
            pltpu.VMEM(((reach + 1) * R, SL, width), F32),
            pltpu.VMEM((FL * COLS, kpad), F32),
            pltpu.VMEM((R, 3 * kpad, C), BF16),
            pltpu.VMEM((R, FA * COLS, C), F32),
            pltpu.VMEM((R, FA * COLS, C), BF16),
            pltpu.VMEM((R, SL * COLS, C), BF16),
            pltpu.VMEM((3, 3, 3, half, C), BF16),
            pltpu.SemaphoreType.DMA((reach + 1, R)),
            pltpu.SemaphoreType.DMA((reach + 1, R)),
            pltpu.SemaphoreType.DMA((reach + 1, R)),
            pltpu.SemaphoreType.DMA((3,)),
            pltpu.SemaphoreType.DMA((R, 3)),
            pltpu.SemaphoreType.DMA((6,)),
        ],
        compiler_params=pltpu.CompilerParams(
            collective_id=0, has_side_effects=True, vmem_limit_bytes=40 * 1024 * 1024
        ),
    )(*[pltpu.with_memory_space_constraint(z, pltpu.HBM) for z in (
        frame_counts,
        latents.reshape(SL, width),
        w_in.reshape(3, 9 * LAT, C),
        gain_in,
        shift_in,
        jnp.swapaxes(w_mid, 3, 4),
        gain_out,
        shift_out,
    )])
    return jnp.swapaxes(raw, 1, 2)[:, None]


def solution(mesh):
    return jax.shard_map(
        shards,
        mesh=mesh,
        in_specs=(
            P(("video", "block"), "band", None),
            P("video"),
            P(),
            P(),
            P(),
            P(None, None, None, None, "chan"),
            P("chan"),
            P("chan"),
        ),
        out_specs=P(("video", "block"), "band", None, "chan"),
        check_vma=False,
    )
```
